32 devices in a mesh: leaf: 8 (over z, y), rows: 4 (over x, core).
Axes of the slice: x: 2, y: 2, z: 4, core: 2. Of those that a mesh axis runs over, the one named last changes fastest.
Arguments:
- samples: bfloat16 [262144, 256], P(('leaf', 'rows')), may hold values from -40 to 40
- row_order: int32 [2048, 128], P(('leaf', 'rows')), may hold values from 0 to 127, each once within a row
- cluster_map: int32 [2048], P(('leaf', 'rows')), may hold values from 0 to 7, as said below
- leaf_sketch: bfloat16 [256, 128], replicated, may hold values from -0.375 to 0.375
- level_sketch: float32 [3, 256, 128], replicated, may hold values from -0.375 to 0.375
Outputs:
- bases: bfloat16 [524288, 128], P(('leaf', 'rows'))
- transfers: float32 [8, 3, 128, 128], P('leaf')
- summaries: float32 [8, 128, 256], P('leaf')
The draws below stay inside these ranges and needn't reach their ends.
Inputs may be any that keep to these rules, and one draw needn't show every extreme that they name: `cluster_map`: the 64 blocks of one device name each cluster at most 16 times; in every draw one cluster is named exactly 16 times on every device.
All inputs are finite; a program needn't handle non-finite values.
Results may differ from the reference program's by a relative error of at most 0.023.
Values may be sent and summed in bfloat16 or wider, within the bound.
A program may use at most 128 MiB of HBM per device.

```python
import math
import jax
import jax.numpy as jnp
from jax import lax

SUB_DEV = 64
BLK = 128
PCOLS = 256
RANK = 128
LEVELS = 3
CLUSTERS = 8
CAPS = 16
BLOCKS = 2048
N_LEAF = 8
N_ROWS = 4


def draw_samples(key, part):
    first, second, third = jax.random.split(jax.random.fold_in(key, 11), 3)
    total_rows = BLOCKS * BLK
    base = jnp.clip(jax.random.normal(first, (total_rows, PCOLS), jnp.float32), -6.0, 6.0)
    mixed = base + 0.6 * jnp.roll(base, 1, axis=1)
    col_scale = jnp.exp(jax.random.uniform(second, (1, PCOLS), jnp.float32, 0.0, math.log(4.0)))
    row_scale = jnp.exp(jax.random.uniform(third, (total_rows, 1), jnp.float32, math.log(0.5), math.log(2.0)))
    return jnp.clip(mixed * col_scale * row_scale, -40.0, 40.0).astype(jnp.bfloat16)


def draw_cluster_map(key, part):
    base_key = jax.random.fold_in(key, 5)
    hottest = jax.random.randint(jax.random.fold_in(base_key, 1), (), 0, CLUSTERS)
    device_count = BLOCKS // SUB_DEV
    device_keys = jax.random.split(jax.random.fold_in(base_key, 2), device_count)

    def one_device(device_key):
        pick_key, order_key = jax.random.split(device_key)
        others = jax.random.permutation(pick_key, (CLUSTERS - 1) * CAPS)[:SUB_DEV - CAPS]
        relative = jnp.concatenate([jnp.zeros((CAPS,), jnp.int32), 1 + others.astype(jnp.int32) // CAPS])
        chosen = (relative + hottest) % CLUSTERS
        return jax.random.permutation(order_key, chosen)
    return jax.vmap(one_device)(device_keys).reshape(BLOCKS).astype(jnp.int32)


def scatter_about(stream_key, extent, deviation, most, kind=jnp.bfloat16):
    result = jax.random.normal(stream_key, extent, jnp.float32) * deviation
    return jnp.minimum(jnp.maximum(result, -most), most).astype(kind)


def setup_inputs(seed: int = 0) -> dict:
    seeds = jax.random.split(jax.random.key(seed), 6)
    samples = draw_samples(jax.random.fold_in(seeds[5], 71), 0)
    row_order = jax.vmap(lambda own: jax.random.permutation(own, BLK))(jax.random.split(seeds[1], BLOCKS)).reshape((BLOCKS, BLK)).astype(jnp.int32)
    cluster_map = draw_cluster_map(jax.random.fold_in(seeds[5], 71), 0)
    leaf_sketch = scatter_about(seeds[3], (PCOLS, RANK), PCOLS ** -0.5, 0.375)
    level_sketch = scatter_about(seeds[4], (LEVELS, PCOLS, RANK), PCOLS ** -0.5, 0.375, jnp.float32)
    return dict(samples=samples, row_order=row_order, cluster_map=cluster_map, leaf_sketch=leaf_sketch, level_sketch=level_sketch)


SHIFT = 0.01

def merge_pair(stacked, sketch_level):
    rows_total = stacked.shape[0]
    rank_cols = sketch_level.shape[1]
    sample_cols = stacked.shape[1]
    projected = jnp.dot(stacked, sketch_level, precision=lax.Precision.HIGHEST)
    gram = jnp.dot(projected.T, projected, precision=lax.Precision.HIGHEST) / rows_total + SHIFT * jnp.eye(rank_cols, dtype=jnp.float32)
    lower_factor = jnp.linalg.cholesky(gram)
    inverse_lower = lax.linalg.triangular_solve(lower_factor, jnp.eye(rank_cols, dtype=jnp.float32), left_side=True, lower=True)
    transfer = jnp.dot(projected, inverse_lower.T, precision=lax.Precision.HIGHEST)
    product = jnp.dot(projected.T, stacked, precision=lax.Precision.HIGHEST)
    parent = jnp.dot(inverse_lower, product, precision=lax.Precision.HIGHEST) * (math.sqrt(sample_cols) / rows_total)
    return (transfer, parent)

def split_apply(sketched, inverse_lower):
    whole = inverse_lower.T
    upper_part = whole.astype(jnp.bfloat16)
    lower_part = (whole - upper_part.astype(jnp.float32)).astype(jnp.bfloat16)
    first = jnp.dot(sketched.astype(jnp.float32), upper_part.astype(jnp.float32), preferred_element_type=jnp.float32)
    second = jnp.dot(sketched.astype(jnp.float32), lower_part.astype(jnp.float32), preferred_element_type=jnp.float32)
    return (first + second).astype(jnp.bfloat16)

def reference(samples, row_order, cluster_map, leaf_sketch, level_sketch):
    devices = N_LEAF * N_ROWS
    blocks = samples.reshape(BLOCKS, BLK, PCOLS)
    ordered = jnp.take_along_axis(blocks, row_order[:, :, None], axis=1)
    maps = cluster_map.reshape(devices, SUB_DEV)
    hits = (maps[:, :, None] == jnp.arange(CLUSTERS, dtype=jnp.int32)[None, None, :]).astype(jnp.int32)
    before = jnp.cumsum(hits, axis=1) - hits
    slot_rank = lax.optimization_barrier(jnp.sum(before * hits, axis=2)).reshape(BLOCKS).astype(jnp.int32)
    device_index = (jnp.arange(BLOCKS, dtype=jnp.int32) // SUB_DEV).astype(jnp.int32)
    source_leaf = device_index // N_ROWS
    source_row = device_index % N_ROWS
    target_device = (cluster_map * N_ROWS + source_row).astype(jnp.int32)
    target_block = (source_leaf * CAPS + slot_rank).astype(jnp.int32)
    buffer = jnp.zeros((devices, CLUSTERS * CAPS, BLK, PCOLS), jnp.bfloat16)
    buffer = buffer.at[target_device, target_block].set(ordered)
    cluster_rows = buffer.reshape(CLUSTERS, N_ROWS * CLUSTERS * CAPS * BLK, PCOLS)
    row_norm = float(N_ROWS * SUB_DEV * BLK)

    def leaf_work(received):
        sketched = jnp.dot(received.astype(jnp.float32), leaf_sketch.astype(jnp.float32), preferred_element_type=jnp.float32).astype(jnp.bfloat16)
        gram = jnp.dot(sketched.T.astype(jnp.float32), sketched.astype(jnp.float32), preferred_element_type=jnp.float32)
        cross = jnp.dot(sketched.T.astype(jnp.float32), received.astype(jnp.float32), preferred_element_type=jnp.float32)
        gram = gram / row_norm + SHIFT * jnp.eye(RANK, dtype=jnp.float32)
        lower_factor = jnp.linalg.cholesky(gram)
        inverse_lower = lax.linalg.triangular_solve(lower_factor, jnp.eye(RANK, dtype=jnp.float32), left_side=True, lower=True)
        basis = split_apply(sketched, inverse_lower)
        summary = jnp.dot(inverse_lower, cross, precision=lax.Precision.HIGHEST) * (math.sqrt(PCOLS) / row_norm)
        return (basis, summary)
    bases, nodes_now = lax.map(leaf_work, cluster_rows)
    cluster_index = jnp.arange(CLUSTERS, dtype=jnp.int32)
    halves = []
    for depth_index in range(LEVELS):
        paired = nodes_now.reshape(-1, 2 * RANK, PCOLS)
        transfer_all, parent_all = jax.vmap(merge_pair, in_axes=(0, None))(paired, level_sketch[depth_index])
        split_all = transfer_all.reshape(-1, 2, RANK, RANK)
        halves.append(split_all[cluster_index >> depth_index + 1, cluster_index >> depth_index & 1])
        nodes_now = parent_all
    summaries = nodes_now[cluster_index >> LEVELS]
    return (bases.reshape(-1, RANK), jnp.stack(halves, axis=1), summaries)
```

```python
import functools
import math

import jax
import jax.numpy as jnp
from jax import lax
from jax.experimental import pallas as pl
from jax.experimental.pallas import tpu as pltpu
from jax.sharding import PartitionSpec as P

LEVELS = 3
SHIFT = 0.01
TILE = 8
GROUP = 4
STEP_BLOCKS = 8
VMEM_BYTES = 56 * 1024 * 1024
MESH = pl.DeviceIdType.MESH
HIGHEST = lax.Precision.HIGHEST


def dot_first(left, right, precision=None):
    return lax.dot_general(
        left,
        right,
        (((0,), (0,)), ((), ())),
        precision=precision,
        preferred_element_type=jnp.float32,
    )


def dot_last(left, right, precision=None):
    return lax.dot_general(
        left,
        right,
        (((1,), (1,)), ((), ())),
        precision=precision,
        preferred_element_type=jnp.float32,
    )


def identity(size):
    rows = lax.broadcasted_iota(jnp.int32, (size, size), 0)
    cols = lax.broadcasted_iota(jnp.int32, (size, size), 1)
    return jnp.where(rows == cols, 1.0, 0.0).astype(jnp.float32)


def inverse_factor(gram):
    size = gram.shape[0]
    row_id = lax.broadcasted_iota(jnp.int32, (size, size), 0)

    def panel(_, carry):
        a, b = carry
        for s in range(0, TILE, GROUP):
            cols = [jnp.broadcast_to(a[:, s + j : s + j + 1], (size, size)) for j in range(GROUP)]
            rows_a = [a[s + j : s + j + 1, :] for j in range(GROUP)]
            rows_b = [b[s + j : s + j + 1, :] for j in range(GROUP)]
            scales = []
            for j in range(GROUP):
                pivot = cols[j][s + j : s + j + 1, :]
                inv = 1.0 / pivot
                scales.append(lax.rsqrt(pivot))
                for i in range(j + 1, GROUP):
                    factor = cols[j][s + i : s + i + 1, :] * inv
                    cols[i] = cols[i] - cols[j] * factor
                    rows_a[i] = rows_a[i] - factor * rows_a[j]
                    rows_b[i] = rows_b[i] - factor * rows_b[j]
                below = jnp.where(row_id > s + j, cols[j], 0.0)
                a = a - below * (rows_a[j] * inv)
                b = b - below * (rows_b[j] * inv)
            for j in range(GROUP):
                b = jnp.where(row_id == s + j, rows_b[j] * scales[j], b)
        a = jnp.concatenate([a[TILE:], jnp.zeros((TILE, size), jnp.float32)], axis=0)
        a = pltpu.roll(a, size - TILE, 1)
        b = jnp.concatenate([b[TILE:], b[:TILE]], axis=0)
        return a, b

    return lax.fori_loop(0, size // TILE, panel, (gram, identity(size)))[1]


def local_kernel(capacity, map_ref, order_ref, x_ref, sketch_ref, packed_ref, sums_ref, count_ref):
    step = pl.program_id(0)
    clusters = sums_ref.shape[0]
    rows = order_ref.shape[1]

    @pl.when(step == 0)
    def _():
        def clear(c, carry):
            count_ref[c] = 0
            sums_ref[c] = jnp.zeros(sums_ref.shape[1:], jnp.float32)
            for j in range(capacity):
                packed_ref[c * capacity + j] = jnp.zeros(packed_ref.shape[1:], jnp.bfloat16)
            return carry

        lax.fori_loop(0, clusters, clear, 0)

    sketched = jnp.dot(x_ref[...], sketch_ref[...], preferred_element_type=jnp.float32).astype(
        jnp.bfloat16
    )
    source = lax.broadcasted_iota(jnp.int32, (rows, rows), 0)
    for i in range(STEP_BLOCKS):
        cluster = map_ref[step * STEP_BLOCKS + i]
        rank = count_ref[cluster]
        count_ref[cluster] = rank + 1
        block = sketched[i * rows : (i + 1) * rows]
        taken = jnp.where(source == order_ref[i : i + 1, :], 1.0, 0.0).astype(jnp.bfloat16)
        packed_ref[cluster * capacity + rank] = dot_first(taken, block).astype(jnp.bfloat16)
        wide = jnp.concatenate([block, x_ref[i * rows : (i + 1) * rows, :]], axis=1)
        sums_ref[cluster] += dot_first(block, wide)


def flip(index, mask):
    return index + mask - 2 * mask * lax.rem(lax.div(index, mask), 2)


def exchange_kernel(
    capacity,
    row_norm,
    leaves,
    lines,
    packed_ref,
    sums_ref,
    level_ref,
    received_ref,
    inverse_ref,
    transfers_ref,
    summary_ref,
    *scratch,
):
    rounds = lines.bit_length() - 1
    halves = scratch[:rounds]
    partial = scratch[rounds : 2 * rounds]
    (
        landed,
        whole,
        nodes,
        siblings,
        block_send,
        block_recv,
        half_send,
        half_recv,
        leaf_send,
        leaf_recv,
        line_send,
        line_recv,
        node_send,
        node_recv,
        own_sem,
    ) = scratch[2 * rounds :]
    me = lax.axis_index("leaf")
    line = lax.axis_index("rows")
    rank = inverse_ref.shape[0]
    sample_cols = level_ref.shape[1]

    barrier = pltpu.get_barrier_semaphore()
    for d in range(1, leaves):
        pl.semaphore_signal(
            barrier, inc=1, device_id=(lax.rem(me + d, leaves), line), device_id_type=MESH
        )
    for d in range(1, lines):
        pl.semaphore_signal(
            barrier, inc=1, device_id=(me, lax.rem(line + d, lines)), device_id_type=MESH
        )
    pl.semaphore_wait(barrier, leaves + lines - 2)

    def remote(src, dst, send, recv, target):
        copy = pltpu.make_async_remote_copy(
            src_ref=src,
            dst_ref=dst,
            send_sem=send,
            recv_sem=recv,
            device_id=target,
            device_id_type=MESH,
        )
        copy.start()
        return copy

    held, start, size = sums_ref, 0, rank
    for k in range(rounds):
        mask = 2**k
        size //= 2
        side = lax.rem(lax.div(line, mask), 2)
        copy = remote(
            held.at[:, pl.ds(pl.multiple_of((1 - side) * size, size), size), :],
            halves[k],
            half_send.at[k],
            half_recv.at[k],
            (me, flip(line, mask)),
        )
        if k == 0:
            own = pltpu.make_async_copy(
                packed_ref.at[pl.ds(me * capacity, capacity)],
                received_ref.at[pl.ds(me * capacity, capacity)],
                own_sem,
            )
            own.start()
        copy.wait()
        kept = pl.multiple_of(side * size, size)
        for c in range(leaves):
            partial[k][c] = held[c, pl.ds(kept, size), :] + halves[k][c]
        held, start = partial[k], start + side * size

    sums = []
    for d in range(1, leaves):
        peer = lax.rem(me + d, leaves)
        sums.append(
            remote(held.at[peer], landed.at[me], leaf_send.at[d], leaf_recv.at[d], (peer, line))
        )
    blocks = []
    for d in sorted(range(1, leaves), key=lambda value: abs(value - leaves // 2)):
        peer = lax.rem(me + d, leaves)
        blocks.append(
            remote(
                packed_ref.at[pl.ds(peer * capacity, capacity)],
                received_ref.at[pl.ds(me * capacity, capacity)],
                block_send.at[d],
                block_recv.at[d],
                (peer, line),
            )
        )
    total = held[me]
    for d in range(1, leaves):
        sums[d - 1].wait()
        total = total + landed[lax.rem(me - d + leaves, leaves)]
    start = pl.multiple_of(start, size)
    whole[pl.ds(start, size), :] = total
    shares = [
        remote(
            whole.at[pl.ds(start, size), :],
            whole.at[pl.ds(start, size), :],
            line_send.at[d],
            line_recv.at[d],
            (me, lax.rem(line + d, lines)),
        )
        for d in range(1, lines)
    ]
    for copy in shares:
        copy.wait()

    eye = identity(rank)
    inverse = inverse_factor(whole[:, :rank] / row_norm + SHIFT * eye)
    inverse_ref[...] = inverse
    nodes[0] = jnp.dot(inverse, whole[:, rank:], precision=HIGHEST) * (
        math.sqrt(sample_cols) / row_norm
    )
    for t in range(LEVELS):
        copy = remote(
            nodes.at[t], siblings.at[t], node_send.at[t], node_recv.at[t], (flip(me, 2**t), line)
        )
        own_node = nodes[t]
        sketch = level_ref[t]
        projected = jnp.dot(own_node, sketch, precision=HIGHEST)
        wide = jnp.concatenate([projected, own_node], axis=1)
        own_product = dot_first(projected, wide, HIGHEST)
        copy.wait()
        other_node = siblings[t]
        other = jnp.dot(other_node, sketch, precision=HIGHEST)
        other_wide = jnp.concatenate([other, other_node], axis=1)
        product = own_product + dot_first(other, other_wide, HIGHEST)
        inverse = inverse_factor(product[:, :rank] / (2 * rank) + SHIFT * eye)
        transfers_ref[t] = dot_last(projected, inverse, HIGHEST)
        parent = jnp.dot(inverse, product[:, rank:], precision=HIGHEST) * (
            math.sqrt(sample_cols) / (2 * rank)
        )
        if t == LEVELS - 1:
            summary_ref[...] = parent
        else:
            nodes[t + 1] = parent

    own.wait()
    for copy in blocks:
        copy.wait()


def basis_kernel(rows_ref, inverse_ref, basis_ref):
    inverse = inverse_ref[...]
    upper = inverse.astype(jnp.bfloat16)
    lower = (inverse - upper.astype(jnp.float32)).astype(jnp.bfloat16)
    rows = rows_ref[...]
    basis_ref[...] = (dot_last(rows, upper) + dot_last(rows, lower)).astype(jnp.bfloat16)


def body(samples, row_order, cluster_map, leaf_sketch, level_sketch):
    block_count = cluster_map.shape[0]
    block_rows = row_order.shape[1]
    sample_cols = samples.shape[1]
    rank = leaf_sketch.shape[1]
    leaves = lax.axis_size("leaf")
    lines = lax.axis_size("rows")
    capacity = 2 * block_count // leaves
    slots = leaves * capacity
    width = rank + sample_cols
    row_norm = float(lines * block_count * block_rows)
    vmem = pl.BlockSpec(memory_space=pltpu.VMEM)
    anywhere = pl.BlockSpec(memory_space=pl.ANY)

    packed, sums = pl.pallas_call(
        functools.partial(local_kernel, capacity),
        grid=(block_count // STEP_BLOCKS,),
        in_specs=[
            pl.BlockSpec(memory_space=pltpu.SMEM),
            pl.BlockSpec((STEP_BLOCKS, block_rows), lambda i: (i, 0)),
            pl.BlockSpec((STEP_BLOCKS * block_rows, sample_cols), lambda i: (i, 0)),
            pl.BlockSpec((sample_cols, rank), lambda i: (0, 0)),
        ],
        out_specs=[
            pl.BlockSpec((slots, block_rows, rank), lambda i: (0, 0, 0)),
            pl.BlockSpec((leaves, rank, width), lambda i: (0, 0, 0)),
        ],
        out_shape=[
            jax.ShapeDtypeStruct((slots, block_rows, rank), jnp.bfloat16),
            jax.ShapeDtypeStruct((leaves, rank, width), jnp.float32),
        ],
        scratch_shapes=[pltpu.SMEM((leaves,), jnp.int32)],
        compiler_params=pltpu.CompilerParams(vmem_limit_bytes=VMEM_BYTES),
        name="sketch_blocks",
    )(cluster_map, row_order, samples, leaf_sketch)

    rounds = lines.bit_length() - 1
    shares = [
        pltpu.VMEM((leaves, rank >> (k + 1), width), jnp.float32) for k in range(rounds)
    ]
    dma = pltpu.SemaphoreType.DMA
    received, inverse, transfers, summary = pl.pallas_call(
        functools.partial(exchange_kernel, capacity, row_norm, leaves, lines),
        in_specs=[anywhere, vmem, vmem],
        out_specs=[anywhere, vmem, vmem, vmem],
        out_shape=[
            jax.ShapeDtypeStruct((slots, block_rows, rank), jnp.bfloat16),
            jax.ShapeDtypeStruct((rank, rank), jnp.float32),
            jax.ShapeDtypeStruct((LEVELS, rank, rank), jnp.float32),
            jax.ShapeDtypeStruct((rank, sample_cols), jnp.float32),
        ],
        scratch_shapes=[
            *shares,
            *shares,
            pltpu.VMEM((leaves, rank // lines, width), jnp.float32),
            pltpu.VMEM((rank, width), jnp.float32),
            pltpu.VMEM((LEVELS, rank, sample_cols), jnp.float32),
            pltpu.VMEM((LEVELS, rank, sample_cols), jnp.float32),
            dma((leaves,)),
            dma((leaves,)),
            dma((rounds,)),
            dma((rounds,)),
            dma((leaves,)),
            dma((leaves,)),
            dma((lines,)),
            dma((lines,)),
            dma((LEVELS,)),
            dma((LEVELS,)),
            dma,
        ],
        compiler_params=pltpu.CompilerParams(
            collective_id=0, has_side_effects=True, vmem_limit_bytes=VMEM_BYTES
        ),
        name="exchange_and_merge",
    )(packed, sums, level_sketch)

    total_rows = slots * block_rows
    tile = min(2048, total_rows)
    basis = pl.pallas_call(
        basis_kernel,
        grid=(total_rows // tile,),
        in_specs=[
            pl.BlockSpec((tile, rank), lambda i: (i, 0)),
            pl.BlockSpec((rank, rank), lambda i: (0, 0)),
        ],
        out_specs=pl.BlockSpec((tile, rank), lambda i: (i, 0)),
        out_shape=jax.ShapeDtypeStruct((total_rows, rank), jnp.bfloat16),
        compiler_params=pltpu.CompilerParams(vmem_limit_bytes=VMEM_BYTES),
        name="leaf_bases",
    )(received.reshape(total_rows, rank), inverse)
    return basis, transfers[None], summary[None]


def solution(mesh):
    in_specs = (P(("leaf", "rows"), None), P(("leaf", "rows"), None), P(("leaf", "rows")), P(), P())
    out_specs = (P(("leaf", "rows"), None), P("leaf", None, None, None), P("leaf", None, None))
    return jax.shard_map(body, mesh=mesh, in_specs=in_specs, out_specs=out_specs, check_vma=False)
```

```python
import functools
import math

import jax
import jax.numpy as jnp
from jax import lax
from jax.experimental import pallas as pl
from jax.experimental.pallas import tpu as pltpu
from jax.sharding import PartitionSpec as P

LEVELS = 3
SHIFT = 0.01
TILE = 8
GROUP = 4
SPLITS = 4
STEP_BLOCKS = 8
VMEM_BYTES = 56 * 1024 * 1024
MESH = pl.DeviceIdType.MESH
HIGHEST = lax.Precision.HIGHEST


def dot_first(left, right, precision=None):
    return lax.dot_general(
        left,
        right,
        (((0,), (0,)), ((), ())),
        precision=precision,
        preferred_element_type=jnp.float32,
    )


def dot_last(left, right, precision=None):
    return lax.dot_general(
        left,
        right,
        (((1,), (1,)), ((), ())),
        precision=precision,
        preferred_element_type=jnp.float32,
    )


def identity(size):
    rows = lax.broadcasted_iota(jnp.int32, (size, size), 0)
    cols = lax.broadcasted_iota(jnp.int32, (size, size), 1)
    return jnp.where(rows == cols, 1.0, 0.0).astype(jnp.float32)


def inverse_factor(gram, between=None):
    size = gram.shape[0]
    row_id = lax.broadcasted_iota(jnp.int32, (TILE, size), 0)

    def panel(_, carry):
        a, b = carry
        first = jnp.zeros((TILE, size), jnp.float32)
        for s in range(0, TILE, GROUP):
            cols = [jnp.broadcast_to(a[:, s + j : s + j + 1], (size, size)) for j in range(GROUP)]
            rows_a = [a[s + j : s + j + 1, :] for j in range(GROUP)]
            rows_b = [b[s + j : s + j + 1, :] for j in range(GROUP)]
            for j in range(GROUP):
                scale = lax.rsqrt(cols[j][s + j : s + j + 1, :])
                inv = scale * scale
                for i in range(j + 1, GROUP):
                    factor = cols[j][s + i : s + i + 1, :] * inv
                    cols[i] = cols[i] - cols[j] * factor
                    rows_a[i] = rows_a[i] - factor * rows_a[j]
                    rows_b[i] = rows_b[i] - factor * rows_b[j]
                top = jnp.where(row_id > s + j, cols[j][:TILE], 0.0)
                below = jnp.concatenate([top, cols[j][TILE:]], axis=0)
                a = a - below * (rows_a[j] * inv)
                b = b - below * (rows_b[j] * inv)
                first = jnp.where(row_id == s + j, rows_b[j] * scale, first)
        a = jnp.concatenate([a[TILE:], jnp.zeros((TILE, size), jnp.float32)], axis=0)
        a = pltpu.roll(a, size - TILE, 1)
        b = jnp.concatenate([b[TILE:], first], axis=0)
        return a, b

    def part(i, carry):
        if between is not None:
            between(i)
        return lax.fori_loop(0, size // (TILE * SPLITS), panel, carry)

    return lax.fori_loop(0, SPLITS, part, (gram, identity(size)))[1]


def local_kernel(capacity, map_ref, order_ref, x_ref, sketch_ref, packed_ref, sums_ref, count_ref):
    step = pl.program_id(0)
    clusters = sums_ref.shape[0]
    rows = order_ref.shape[1]

    @pl.when(step == 0)
    def _():
        def clear(c, carry):
            count_ref[c] = 0
            sums_ref[c] = jnp.zeros(sums_ref.shape[1:], jnp.float32)
            for j in range(capacity):
                packed_ref[c * capacity + j] = jnp.zeros(packed_ref.shape[1:], jnp.bfloat16)
            return carry

        lax.fori_loop(0, clusters, clear, 0)

    sketched = jnp.dot(x_ref[...], sketch_ref[...], preferred_element_type=jnp.float32).astype(
        jnp.bfloat16
    )
    source = lax.broadcasted_iota(jnp.int32, (rows, rows), 0)
    for i in range(STEP_BLOCKS):
        cluster = map_ref[step * STEP_BLOCKS + i]
        rank = count_ref[cluster]
        count_ref[cluster] = rank + 1
        block = sketched[i * rows : (i + 1) * rows]
        taken = jnp.where(source == order_ref[i : i + 1, :], 1.0, 0.0).astype(jnp.bfloat16)
        packed_ref[cluster * capacity + rank] = dot_first(taken, block).astype(jnp.bfloat16)
        wide = jnp.concatenate([block, x_ref[i * rows : (i + 1) * rows, :]], axis=1)
        sums_ref[cluster] += dot_first(block, wide)


def flip(index, mask):
    return index + mask - 2 * mask * lax.rem(lax.div(index, mask), 2)


def exchange_kernel(
    capacity,
    row_norm,
    leaves,
    lines,
    packed_ref,
    sums_ref,
    level_ref,
    received_ref,
    inverse_ref,
    transfers_ref,
    summary_ref,
    *scratch,
):
    rounds = lines.bit_length() - 1
    halves = scratch[:rounds]
    partial = scratch[rounds : 2 * rounds]
    (
        landed,
        whole,
        nodes,
        siblings,
        block_send,
        block_recv,
        half_send,
        half_recv,
        leaf_send,
        leaf_recv,
        line_send,
        line_recv,
        node_send,
        node_recv,
        own_sem,
    ) = scratch[2 * rounds :]
    me = lax.axis_index("leaf")
    line = lax.axis_index("rows")
    rank = inverse_ref.shape[0]
    sample_cols = level_ref.shape[1]

    barrier = pltpu.get_barrier_semaphore()
    for d in range(1, leaves):
        pl.semaphore_signal(
            barrier, inc=1, device_id=(lax.rem(me + d, leaves), line), device_id_type=MESH
        )
    for d in range(1, lines):
        pl.semaphore_signal(
            barrier, inc=1, device_id=(me, lax.rem(line + d, lines)), device_id_type=MESH
        )
    pl.semaphore_wait(barrier, leaves + lines - 2)

    def remote(src, dst, send, recv, target):
        copy = pltpu.make_async_remote_copy(
            src_ref=src,
            dst_ref=dst,
            send_sem=send,
            recv_sem=recv,
            device_id=target,
            device_id_type=MESH,
        )
        copy.start()
        return copy

    pieces = max(1, capacity // 4)
    depth = capacity // pieces
    chunks = (leaves - 1) * pieces
    per = max(1, chunks // (5 + LEVELS + SPLITS * (LEVELS + 1)))
    after_sums = 5 * per
    first = chunks - per * (5 + LEVELS + SPLITS * (LEVELS + 1))

    def chunk(i):
        d = 1 + lax.rem(i, leaves - 1)
        offset = lax.div(i, leaves - 1) * depth
        peer = lax.rem(me + d, leaves)
        return pltpu.make_async_remote_copy(
            src_ref=packed_ref.at[pl.ds(peer * capacity + offset, depth)],
            dst_ref=received_ref.at[pl.ds(me * capacity + offset, depth)],
            send_sem=block_send.at[i],
            recv_sem=block_recv.at[i],
            device_id=(peer, line),
            device_id_type=MESH,
        )

    def send_chunks(base, count):
        def send(i, carry):
            chunk(base + i).start()
            return carry

        lax.fori_loop(0, count, send, 0)

    send_chunks(0, first)

    held, start, size = sums_ref, 0, rank
    for k in range(rounds):
        mask = 2**k
        size //= 2
        side = lax.rem(lax.div(line, mask), 2)
        copy = remote(
            held.at[:, pl.ds(pl.multiple_of((1 - side) * size, size), size), :],
            halves[k],
            half_send.at[k],
            half_recv.at[k],
            (me, flip(line, mask)),
        )
        if k == 0:
            own = pltpu.make_async_copy(
                packed_ref.at[pl.ds(me * capacity, capacity)],
                received_ref.at[pl.ds(me * capacity, capacity)],
                own_sem,
            )
            own.start()
        copy.wait()
        kept = pl.multiple_of(side * size, size)
        for c in range(leaves):
            partial[k][c] = held[c, pl.ds(kept, size), :] + halves[k][c]
        held, start = partial[k], start + side * size

    sums = []
    for d in range(1, leaves):
        peer = lax.rem(me + d, leaves)
        sums.append(
            remote(held.at[peer], landed.at[me], leaf_send.at[d], leaf_recv.at[d], (peer, line))
        )
    send_chunks(first, after_sums)
    total = held[me]
    for d in range(1, leaves):
        sums[d - 1].wait()
        total = total + landed[lax.rem(me - d + leaves, leaves)]
    start = pl.multiple_of(start, size)
    whole[pl.ds(start, size), :] = total
    shares = [
        remote(
            whole.at[pl.ds(start, size), :],
            whole.at[pl.ds(start, size), :],
            line_send.at[d],
            line_recv.at[d],
            (me, lax.rem(line + d, lines)),
        )
        for d in range(1, lines)
    ]
    for copy in shares:
        copy.wait()

    eye = identity(rank)
    base = first + after_sums
    inverse = inverse_factor(
        whole[:, :rank] / row_norm + SHIFT * eye,
        lambda i, base=base: send_chunks(base + i * per, per),
    )
    base += SPLITS * per
    inverse_ref[...] = inverse
    nodes[0] = jnp.dot(inverse, whole[:, rank:], precision=HIGHEST) * (
        math.sqrt(sample_cols) / row_norm
    )
    for t in range(LEVELS):
        copy = remote(
            nodes.at[t], siblings.at[t], node_send.at[t], node_recv.at[t], (flip(me, 2**t), line)
        )
        send_chunks(base, per)
        base += per
        own_node = nodes[t]
        sketch = level_ref[t]
        projected = jnp.dot(own_node, sketch, precision=HIGHEST)
        wide = jnp.concatenate([projected, own_node], axis=1)
        own_product = dot_first(projected, wide, HIGHEST)
        copy.wait()
        other_node = siblings[t]
        other = jnp.dot(other_node, sketch, precision=HIGHEST)
        other_wide = jnp.concatenate([other, other_node], axis=1)
        product = own_product + dot_first(other, other_wide, HIGHEST)
        inverse = inverse_factor(
            product[:, :rank] / (2 * rank) + SHIFT * eye,
            lambda i, base=base: send_chunks(base + i * per, per),
        )
        base += SPLITS * per
        transfers_ref[t] = dot_last(projected, inverse, HIGHEST)
        parent = jnp.dot(inverse, product[:, rank:], precision=HIGHEST) * (
            math.sqrt(sample_cols) / (2 * rank)
        )
        if t == LEVELS - 1:
            summary_ref[...] = parent
        else:
            nodes[t + 1] = parent

    own.wait()

    def finish(i, carry):
        chunk(i).wait()
        return carry

    lax.fori_loop(0, chunks, finish, 0)


def basis_kernel(rows_ref, inverse_ref, basis_ref):
    inverse = inverse_ref[...]
    upper = inverse.astype(jnp.bfloat16)
    lower = (inverse - upper.astype(jnp.float32)).astype(jnp.bfloat16)
    both = jnp.concatenate([upper, lower], axis=1)
    rows = rows_ref[...]
    twice = jnp.concatenate([rows, rows], axis=1)
    basis_ref[...] = dot_last(twice, both).astype(jnp.bfloat16)


def body(samples, row_order, cluster_map, leaf_sketch, level_sketch):
    block_count = cluster_map.shape[0]
    block_rows = row_order.shape[1]
    sample_cols = samples.shape[1]
    rank = leaf_sketch.shape[1]
    leaves = lax.axis_size("leaf")
    lines = lax.axis_size("rows")
    capacity = 2 * block_count // leaves
    slots = leaves * capacity
    width = rank + sample_cols
    row_norm = float(lines * block_count * block_rows)
    vmem = pl.BlockSpec(memory_space=pltpu.VMEM)
    anywhere = pl.BlockSpec(memory_space=pl.ANY)

    packed, sums = pl.pallas_call(
        functools.partial(local_kernel, capacity),
        grid=(block_count // STEP_BLOCKS,),
        in_specs=[
            pl.BlockSpec(memory_space=pltpu.SMEM),
            pl.BlockSpec((STEP_BLOCKS, block_rows), lambda i: (i, 0)),
            pl.BlockSpec((STEP_BLOCKS * block_rows, sample_cols), lambda i: (i, 0)),
            pl.BlockSpec((sample_cols, rank), lambda i: (0, 0)),
        ],
        out_specs=[
            pl.BlockSpec((slots, block_rows, rank), lambda i: (0, 0, 0)),
            pl.BlockSpec((leaves, rank, width), lambda i: (0, 0, 0)),
        ],
        out_shape=[
            jax.ShapeDtypeStruct((slots, block_rows, rank), jnp.bfloat16),
            jax.ShapeDtypeStruct((leaves, rank, width), jnp.float32),
        ],
        scratch_shapes=[pltpu.SMEM((leaves,), jnp.int32)],
        compiler_params=pltpu.CompilerParams(vmem_limit_bytes=VMEM_BYTES),
        name="sketch_blocks",
    )(cluster_map, row_order, samples, leaf_sketch)

    rounds = lines.bit_length() - 1
    shares = [
        pltpu.VMEM((leaves, rank >> (k + 1), width), jnp.float32) for k in range(rounds)
    ]
    dma = pltpu.SemaphoreType.DMA
    chunks = (leaves - 1) * max(1, capacity // 4)
    received, inverse, transfers, summary = pl.pallas_call(
        functools.partial(exchange_kernel, capacity, row_norm, leaves, lines),
        in_specs=[anywhere, vmem, vmem],
        out_specs=[anywhere, vmem, vmem, vmem],
        out_shape=[
            jax.ShapeDtypeStruct((slots, block_rows, rank), jnp.bfloat16),
            jax.ShapeDtypeStruct((rank, rank), jnp.float32),
            jax.ShapeDtypeStruct((LEVELS, rank, rank), jnp.float32),
            jax.ShapeDtypeStruct((rank, sample_cols), jnp.float32),
        ],
        scratch_shapes=[
            *shares,
            *shares,
            pltpu.VMEM((leaves, rank // lines, width), jnp.float32),
            pltpu.VMEM((rank, width), jnp.float32),
            pltpu.VMEM((LEVELS, rank, sample_cols), jnp.float32),
            pltpu.VMEM((LEVELS, rank, sample_cols), jnp.float32),
            dma((chunks,)),
            dma((chunks,)),
            dma((rounds,)),
            dma((rounds,)),
            dma((leaves,)),
            dma((leaves,)),
            dma((lines,)),
            dma((lines,)),
            dma((LEVELS,)),
            dma((LEVELS,)),
            dma,
        ],
        compiler_params=pltpu.CompilerParams(
            collective_id=0, has_side_effects=True, vmem_limit_bytes=VMEM_BYTES
        ),
        name="exchange_and_merge",
    )(packed, sums, level_sketch)

    total_rows = slots * block_rows
    tile = min(2048, total_rows)
    basis = pl.pallas_call(
        basis_kernel,
        grid=(total_rows // tile,),
        in_specs=[
            pl.BlockSpec((tile, rank), lambda i: (i, 0)),
            pl.BlockSpec((rank, rank), lambda i: (0, 0)),
        ],
        out_specs=pl.BlockSpec((tile, rank), lambda i: (i, 0)),
        out_shape=jax.ShapeDtypeStruct((total_rows, rank), jnp.bfloat16),
        compiler_params=pltpu.CompilerParams(vmem_limit_bytes=VMEM_BYTES),
        name="leaf_bases",
    )(received.reshape(total_rows, rank), inverse)
    return basis, transfers[None], summary[None]


def solution(mesh):
    in_specs = (P(("leaf", "rows"), None), P(("leaf", "rows"), None), P(("leaf", "rows")), P(), P())
    out_specs = (P(("leaf", "rows"), None), P("leaf", None, None, None), P("leaf", None, None))
    return jax.shard_map(body, mesh=mesh, in_specs=in_specs, out_specs=out_specs, check_vma=False)
```

```python
import functools
import math

import jax
import jax.numpy as jnp
from jax import lax
from jax.experimental import pallas as pl
from jax.experimental.pallas import tpu as pltpu
from jax.sharding import PartitionSpec as P

LEVELS = 3
SHIFT = 0.01
TILE = 8
GROUP = 4
SPLITS = 4
STEP_BLOCKS = 8
BASIS_PARTS = 16
VMEM_BYTES = 56 * 1024 * 1024
MESH = pl.DeviceIdType.MESH
HIGHEST = lax.Precision.HIGHEST


def dot_first(left, right, precision=None):
    return lax.dot_general(
        left,
        right,
        (((0,), (0,)), ((), ())),
        precision=precision,
        preferred_element_type=jnp.float32,
    )


def dot_last(left, right, precision=None):
    return lax.dot_general(
        left,
        right,
        (((1,), (1,)), ((), ())),
        precision=precision,
        preferred_element_type=jnp.float32,
    )


def identity(size):
    rows = lax.broadcasted_iota(jnp.int32, (size, size), 0)
    cols = lax.broadcasted_iota(jnp.int32, (size, size), 1)
    return jnp.where(rows == cols, 1.0, 0.0).astype(jnp.float32)


def inverse_factor(gram, between=None):
    size = gram.shape[0]
    row_id = lax.broadcasted_iota(jnp.int32, (TILE, size), 0)

    def panel(_, carry):
        a, b = carry
        first = jnp.zeros((TILE, size), jnp.float32)
        for s in range(0, TILE, GROUP):
            cols = [jnp.broadcast_to(a[:, s + j : s + j + 1], (size, size)) for j in range(GROUP)]
            rows_a = [a[s + j : s + j + 1, :] for j in range(GROUP)]
            rows_b = [b[s + j : s + j + 1, :] for j in range(GROUP)]
            for j in range(GROUP):
                scale = lax.rsqrt(cols[j][s + j : s + j + 1, :])
                inv = scale * scale
                for i in range(j + 1, GROUP):
                    factor = cols[j][s + i : s + i + 1, :] * inv
                    cols[i] = cols[i] - cols[j] * factor
                    rows_a[i] = rows_a[i] - factor * rows_a[j]
                    rows_b[i] = rows_b[i] - factor * rows_b[j]
                top = jnp.where(row_id > s + j, cols[j][:TILE], 0.0)
                below = jnp.concatenate([top, cols[j][TILE:]], axis=0)
                a = a - below * (rows_a[j] * inv)
                b = b - below * (rows_b[j] * inv)
                first = jnp.where(row_id == s + j, rows_b[j] * scale, first)
        a = jnp.concatenate([a[TILE:], jnp.zeros((TILE, size), jnp.float32)], axis=0)
        a = pltpu.roll(a, size - TILE, 1)
        b = jnp.concatenate([b[TILE:], first], axis=0)
        return a, b

    def part(i, carry):
        if between is not None:
            between(i)
        return lax.fori_loop(0, size // (TILE * SPLITS), panel, carry)

    return lax.fori_loop(0, SPLITS, part, (gram, identity(size)))[1]


def run(count, work):
    def one(i, carry):
        work(i)
        return carry

    lax.fori_loop(0, count, one, 0)


def local_kernel(
    capacity,
    map_ref,
    order_ref,
    x_ref,
    sketch_ref,
    packed_ref,
    sums_ref,
    x_buf,
    packed_buf,
    sums_buf,
    count_ref,
    in_sem,
    packed_sem,
    sums_sem,
):
    clusters = sums_ref.shape[0]
    block_count, rows = order_ref.shape
    tall = STEP_BLOCKS * rows

    def load(step):
        span = pl.ds(pl.multiple_of(step * tall, tall), tall)
        return pltpu.make_async_copy(x_ref.at[span], x_buf.at[span], in_sem.at[step])

    def store_packed(c):
        span = pl.ds(c * capacity, capacity)
        return pltpu.make_async_copy(packed_buf.at[span], packed_ref.at[span], packed_sem.at[c])

    def store_sums(c):
        return pltpu.make_async_copy(sums_buf.at[c], sums_ref.at[c], sums_sem.at[c])

    def clear(c):
        count_ref[c] = 0
        sums_buf[c] = jnp.zeros(sums_buf.shape[1:], jnp.float32)
        for j in range(capacity):
            packed_buf[c * capacity + j] = jnp.zeros(packed_buf.shape[1:], jnp.bfloat16)

    run(block_count // STEP_BLOCKS, lambda step: load(step).start())
    run(clusters, clear)
    source = lax.broadcasted_iota(jnp.int32, (rows, rows), 0)

    def work(step):
        load(step).wait()
        x = x_buf[pl.ds(pl.multiple_of(step * tall, tall), tall), :]
        order = order_ref[pl.ds(pl.multiple_of(step * STEP_BLOCKS, STEP_BLOCKS), STEP_BLOCKS), :]
        sketched = jnp.dot(x, sketch_ref[...], preferred_element_type=jnp.float32).astype(
            jnp.bfloat16
        )
        for i in range(STEP_BLOCKS):
            cluster = map_ref[step * STEP_BLOCKS + i]
            rank = count_ref[cluster]
            count_ref[cluster] = rank + 1
            block = sketched[i * rows : (i + 1) * rows]
            taken = jnp.where(source == order[i : i + 1, :], 1.0, 0.0).astype(jnp.bfloat16)
            packed_buf[cluster * capacity + rank] = dot_first(taken, block).astype(jnp.bfloat16)
            wide = jnp.concatenate([block, x[i * rows : (i + 1) * rows, :]], axis=1)
            sums_buf[cluster] += dot_first(block, wide)

    run(block_count // STEP_BLOCKS, work)
    run(clusters, lambda c: store_sums(c).start())
    run(clusters, lambda c: store_packed(c).start())
    run(clusters, lambda c: store_sums(c).wait())
    run(clusters, lambda c: store_packed(c).wait())


def flip(index, mask):
    return index + mask - 2 * mask * lax.rem(lax.div(index, mask), 2)


def exchange_kernel(
    capacity,
    row_norm,
    leaves,
    lines,
    packed_ref,
    sums_ref,
    level_ref,
    received_ref,
    inverse_ref,
    transfers_ref,
    summary_ref,
    *scratch,
):
    rounds = lines.bit_length() - 1
    halves = scratch[:rounds]
    partial = scratch[rounds : 2 * rounds]
    (
        landed,
        whole,
        nodes,
        siblings,
        block_send,
        block_recv,
        half_send,
        half_recv,
        leaf_send,
        leaf_recv,
        line_send,
        line_recv,
        node_send,
        node_recv,
        own_sem,
    ) = scratch[2 * rounds :]
    me = lax.axis_index("leaf")
    line = lax.axis_index("rows")
    rank = inverse_ref.shape[0]
    sample_cols = level_ref.shape[1]

    barrier = pltpu.get_barrier_semaphore()
    for d in range(1, leaves):
        pl.semaphore_signal(
            barrier, inc=1, device_id=(lax.rem(me + d, leaves), line), device_id_type=MESH
        )
    for d in range(1, lines):
        pl.semaphore_signal(
            barrier, inc=1, device_id=(me, lax.rem(line + d, lines)), device_id_type=MESH
        )
    pl.semaphore_wait(barrier, leaves + lines - 2)

    def remote(src, dst, send, recv, target):
        copy = pltpu.make_async_remote_copy(
            src_ref=src,
            dst_ref=dst,
            send_sem=send,
            recv_sem=recv,
            device_id=target,
            device_id_type=MESH,
        )
        copy.start()
        return copy

    pieces = max(1, capacity // 4)
    depth = capacity // pieces
    chunks = (leaves - 1) * pieces
    per = max(1, chunks // (5 + LEVELS + SPLITS * (LEVELS + 1)))
    after_sums = 5 * per
    first = chunks - per * (4 + LEVELS + SPLITS * LEVELS)

    def chunk(i):
        d = 1 + lax.rem(i, leaves - 1)
        offset = lax.div(i, leaves - 1) * depth
        peer = lax.rem(me + d, leaves)
        return pltpu.make_async_remote_copy(
            src_ref=packed_ref.at[pl.ds(peer * capacity + offset, depth)],
            dst_ref=received_ref.at[pl.ds(me * capacity + offset, depth)],
            send_sem=block_send.at[i],
            recv_sem=block_recv.at[i],
            device_id=(peer, line),
            device_id_type=MESH,
        )

    def send_chunks(base, count):
        run(count, lambda i: chunk(base + i).start())

    send_chunks(0, first)

    held, start, size = sums_ref, 0, rank
    for k in range(rounds):
        mask = 2**k
        size //= 2
        side = lax.rem(lax.div(line, mask), 2)
        copy = remote(
            held.at[:, pl.ds(pl.multiple_of((1 - side) * size, size), size), :],
            halves[k],
            half_send.at[k],
            half_recv.at[k],
            (me, flip(line, mask)),
        )
        if k == 0:
            own = pltpu.make_async_copy(
                packed_ref.at[pl.ds(me * capacity, capacity)],
                received_ref.at[pl.ds(me * capacity, capacity)],
                own_sem,
            )
            own.start()
        copy.wait()
        kept = pl.multiple_of(side * size, size)
        for c in range(leaves):
            partial[k][c] = held[c, pl.ds(kept, size), :] + halves[k][c]
        held, start = partial[k], start + side * size

    sums = []
    for d in range(1, leaves):
        peer = lax.rem(me + d, leaves)
        sums.append(
            remote(held.at[peer], landed.at[me], leaf_send.at[d], leaf_recv.at[d], (peer, line))
        )
    send_chunks(first, after_sums)
    total = held[me]
    for d in range(1, leaves):
        sums[d - 1].wait()
        total = total + landed[lax.rem(me - d + leaves, leaves)]
    start = pl.multiple_of(start, size)
    whole[pl.ds(start, size), :] = total
    shares = [
        remote(
            whole.at[pl.ds(start, size), :],
            whole.at[pl.ds(start, size), :],
            line_send.at[d],
            line_recv.at[d],
            (me, lax.rem(line + d, lines)),
        )
        for d in range(1, lines)
    ]
    for copy in shares:
        copy.wait()

    eye = identity(rank)
    base = first + after_sums
    inverse = inverse_factor(
        whole[:, :rank] / row_norm + SHIFT * eye,
        lambda i, base=base: send_chunks(base + i * per, per),
    )
    base += SPLITS * per
    inverse_ref[...] = inverse
    nodes[0] = jnp.dot(inverse, whole[:, rank:], precision=HIGHEST) * (
        math.sqrt(sample_cols) / row_norm
    )
    for t in range(LEVELS):
        copy = remote(
            nodes.at[t], siblings.at[t], node_send.at[t], node_recv.at[t], (flip(me, 2**t), line)
        )
        busy = t < LEVELS - 1
        if busy:
            send_chunks(base, per)
            base += per
        own_node = nodes[t]
        sketch = level_ref[t]
        projected = jnp.dot(own_node, sketch, precision=HIGHEST)
        wide = jnp.concatenate([projected, own_node], axis=1)
        own_product = dot_first(projected, wide, HIGHEST)
        copy.wait()
        other_node = siblings[t]
        other = jnp.dot(other_node, sketch, precision=HIGHEST)
        other_wide = jnp.concatenate([other, other_node], axis=1)
        product = own_product + dot_first(other, other_wide, HIGHEST)
        inverse = inverse_factor(
            product[:, :rank] / (2 * rank) + SHIFT * eye,
            (lambda i, base=base: send_chunks(base + i * per, per)) if busy else None,
        )
        base += SPLITS * per
        transfers_ref[t] = dot_last(projected, inverse, HIGHEST)
        parent = jnp.dot(inverse, product[:, rank:], precision=HIGHEST) * (
            math.sqrt(sample_cols) / (2 * rank)
        )
        if t == LEVELS - 1:
            summary_ref[...] = parent
        else:
            nodes[t + 1] = parent

    own.wait()
    run(chunks, lambda i: chunk(i).wait())


def basis_kernel(rows_ref, inverse_ref, basis_ref, in_buf, out_buf, in_sem, out_sem):
    tall = rows_ref.shape[0] // BASIS_PARTS

    def span(i):
        return pl.ds(pl.multiple_of(i * tall, tall), tall)

    def load(i):
        return pltpu.make_async_copy(rows_ref.at[span(i)], in_buf.at[span(i)], in_sem.at[i])

    def store(i):
        return pltpu.make_async_copy(out_buf.at[span(i)], basis_ref.at[span(i)], out_sem.at[i])

    run(BASIS_PARTS, lambda i: load(i).start())
    inverse = inverse_ref[...]
    upper = inverse.astype(jnp.bfloat16)
    lower = (inverse - upper.astype(jnp.float32)).astype(jnp.bfloat16)
    both = jnp.concatenate([upper.T, lower.T], axis=0)

    def work(i):
        load(i).wait()
        rows = in_buf[span(i), :]
        twice = jnp.concatenate([rows, rows], axis=1)
        out_buf[span(i), :] = jnp.dot(twice, both, preferred_element_type=jnp.float32).astype(
            jnp.bfloat16
        )
        store(i).start()

    run(BASIS_PARTS, work)
    run(BASIS_PARTS, lambda i: store(i).wait())


def body(samples, row_order, cluster_map, leaf_sketch, level_sketch):
    block_count = cluster_map.shape[0]
    block_rows = row_order.shape[1]
    sample_cols = samples.shape[1]
    rank = leaf_sketch.shape[1]
    leaves = lax.axis_size("leaf")
    lines = lax.axis_size("rows")
    capacity = 2 * block_count // leaves
    slots = leaves * capacity
    width = rank + sample_cols
    row_norm = float(lines * block_count * block_rows)
    vmem = pl.BlockSpec(memory_space=pltpu.VMEM)
    anywhere = pl.BlockSpec(memory_space=pl.ANY)
    dma = pltpu.SemaphoreType.DMA

    packed, sums = pl.pallas_call(
        functools.partial(local_kernel, capacity),
        in_specs=[pl.BlockSpec(memory_space=pltpu.SMEM), vmem, anywhere, vmem],
        out_specs=[anywhere, anywhere],
        out_shape=[
            jax.ShapeDtypeStruct((slots, block_rows, rank), jnp.bfloat16),
            jax.ShapeDtypeStruct((leaves, rank, width), jnp.float32),
        ],
        scratch_shapes=[
            pltpu.VMEM((block_count * block_rows, sample_cols), jnp.bfloat16),
            pltpu.VMEM((slots, block_rows, rank), jnp.bfloat16),
            pltpu.VMEM((leaves, rank, width), jnp.float32),
            pltpu.SMEM((leaves,), jnp.int32),
            dma((block_count // STEP_BLOCKS,)),
            dma((leaves,)),
            dma((leaves,)),
        ],
        compiler_params=pltpu.CompilerParams(vmem_limit_bytes=VMEM_BYTES),
        name="sketch_blocks",
    )(cluster_map, row_order, samples, leaf_sketch)

    rounds = lines.bit_length() - 1
    shares = [
        pltpu.VMEM((leaves, rank >> (k + 1), width), jnp.float32) for k in range(rounds)
    ]
    chunks = (leaves - 1) * max(1, capacity // 4)
    received, inverse, transfers, summary = pl.pallas_call(
        functools.partial(exchange_kernel, capacity, row_norm, leaves, lines),
        in_specs=[anywhere, vmem, vmem],
        out_specs=[anywhere, vmem, vmem, vmem],
        out_shape=[
            jax.ShapeDtypeStruct((slots, block_rows, rank), jnp.bfloat16),
            jax.ShapeDtypeStruct((rank, rank), jnp.float32),
            jax.ShapeDtypeStruct((LEVELS, rank, rank), jnp.float32),
            jax.ShapeDtypeStruct((rank, sample_cols), jnp.float32),
        ],
        scratch_shapes=[
            *shares,
            *shares,
            pltpu.VMEM((leaves, rank // lines, width), jnp.float32),
            pltpu.VMEM((rank, width), jnp.float32),
            pltpu.VMEM((LEVELS, rank, sample_cols), jnp.float32),
            pltpu.VMEM((LEVELS, rank, sample_cols), jnp.float32),
            dma((chunks,)),
            dma((chunks,)),
            dma((rounds,)),
            dma((rounds,)),
            dma((leaves,)),
            dma((leaves,)),
            dma((lines,)),
            dma((lines,)),
            dma((LEVELS,)),
            dma((LEVELS,)),
            dma,
        ],
        compiler_params=pltpu.CompilerParams(
            collective_id=0, has_side_effects=True, vmem_limit_bytes=VMEM_BYTES
        ),
        name="exchange_and_merge",
    )(packed, sums, level_sketch)

    total_rows = slots * block_rows
    basis = pl.pallas_call(
        basis_kernel,
        in_specs=[anywhere, vmem],
        out_specs=anywhere,
        out_shape=jax.ShapeDtypeStruct((total_rows, rank), jnp.bfloat16),
        scratch_shapes=[
            pltpu.VMEM((total_rows, rank), jnp.bfloat16),
            pltpu.VMEM((total_rows, rank), jnp.bfloat16),
            dma((BASIS_PARTS,)),
            dma((BASIS_PARTS,)),
        ],
        compiler_params=pltpu.CompilerParams(vmem_limit_bytes=VMEM_BYTES),
        name="leaf_bases",
    )(received.reshape(total_rows, rank), inverse)
    return basis, transfers[None], summary[None]


def solution(mesh):
    in_specs = (P(("leaf", "rows"), None), P(("leaf", "rows"), None), P(("leaf", "rows")), P(), P())
    out_specs = (P(("leaf", "rows"), None), P("leaf", None, None, None), P("leaf", None, None))
    return jax.shard_map(body, mesh=mesh, in_specs=in_specs, out_specs=out_specs, check_vma=False)
```

```python
import functools
import math

import jax
import jax.numpy as jnp
from jax import lax
from jax.experimental import pallas as pl
from jax.experimental.pallas import tpu as pltpu
from jax.sharding import PartitionSpec as P

LEVELS = 3
SHIFT = 0.01
TILE = 8
GROUP = 4
SPLITS = 4
STEP_BLOCKS = 8
BASIS_PARTS = 16
VMEM_BYTES = 56 * 1024 * 1024
MESH = pl.DeviceIdType.MESH
HIGHEST = lax.Precision.HIGHEST


def dot_first(left, right, precision=None):
    return lax.dot_general(
        left,
        right,
        (((0,), (0,)), ((), ())),
        precision=precision,
        preferred_element_type=jnp.float32,
    )


def dot_last(left, right, precision=None):
    return lax.dot_general(
        left,
        right,
        (((1,), (1,)), ((), ())),
        precision=precision,
        preferred_element_type=jnp.float32,
    )


def identity(size):
    rows = lax.broadcasted_iota(jnp.int32, (size, size), 0)
    cols = lax.broadcasted_iota(jnp.int32, (size, size), 1)
    return jnp.where(rows == cols, 1.0, 0.0).astype(jnp.float32)


def inverse_factor(gram, between=None):
    size = gram.shape[0]
    row_id = lax.broadcasted_iota(jnp.int32, (TILE, size), 0)

    def panel(_, carry):
        a, b = carry
        first = jnp.zeros((TILE, size), jnp.float32)
        for s in range(0, TILE, GROUP):
            cols = [jnp.broadcast_to(a[:, s + j : s + j + 1], (size, size)) for j in range(GROUP)]
            rows_a = [a[s + j : s + j + 1, :] for j in range(GROUP)]
            rows_b = [b[s + j : s + j + 1, :] for j in range(GROUP)]
            for j in range(GROUP):
                scale = lax.rsqrt(cols[j][s + j : s + j + 1, :])
                inv = scale * scale
                for i in range(j + 1, GROUP):
                    factor = cols[j][s + i : s + i + 1, :] * inv
                    cols[i] = cols[i] - cols[j] * factor
                    rows_a[i] = rows_a[i] - factor * rows_a[j]
                    rows_b[i] = rows_b[i] - factor * rows_b[j]
                top = jnp.where(row_id > s + j, cols[j][:TILE], 0.0)
                below = jnp.concatenate([top, cols[j][TILE:]], axis=0)
                a = a - below * (rows_a[j] * inv)
                b = b - below * (rows_b[j] * inv)
                first = jnp.where(row_id == s + j, rows_b[j] * scale, first)
        a = jnp.concatenate([a[TILE:], jnp.zeros((TILE, size), jnp.float32)], axis=0)
        a = pltpu.roll(a, size - TILE, 1)
        b = jnp.concatenate([b[TILE:], first], axis=0)
        return a, b

    def part(i, carry):
        if between is not None:
            between(i)
        return lax.fori_loop(0, size // (TILE * SPLITS), panel, carry)

    return lax.fori_loop(0, SPLITS, part, (gram, identity(size)))[1]


def shares_of(capacity):
    if capacity % 16:
        return capacity, 0
    return 3 * capacity // 4, 3 * capacity // 8


def run(count, work):
    def one(i, carry):
        work(i)
        return carry

    lax.fori_loop(0, count, one, 0)


def local_kernel(
    capacity,
    map_ref,
    order_ref,
    x_ref,
    sketch_ref,
    packed_ref,
    sums_ref,
    extra_ref,
    table_ref,
    x_buf,
    packed_buf,
    sums_buf,
    count_ref,
    in_sem,
    packed_sem,
    sums_sem,
):
    regular, spare = shares_of(capacity)
    clusters = sums_ref.shape[0]
    block_count, rows = order_ref.shape
    tall = STEP_BLOCKS * rows

    def load(step):
        span = pl.ds(pl.multiple_of(step * tall, tall), tall)
        return pltpu.make_async_copy(x_ref.at[span], x_buf.at[span], in_sem.at[step])

    def store_packed(c):
        span = pl.ds(c * capacity, capacity)
        return pltpu.make_async_copy(packed_buf.at[span], packed_ref.at[span], packed_sem.at[c])

    def store_sums(c):
        return pltpu.make_async_copy(sums_buf.at[c], sums_ref.at[c], sums_sem.at[c])

    def clear(c):
        count_ref[c] = 0
        sums_buf[c] = jnp.zeros(sums_buf.shape[1:], jnp.float32)
        for j in range(capacity):
            packed_buf[c * capacity + j] = jnp.zeros(packed_buf.shape[1:], jnp.bfloat16)

    run(block_count // STEP_BLOCKS, lambda step: load(step).start())
    run(clusters, clear)
    extra_ref[...] = jnp.zeros(extra_ref.shape, jnp.bfloat16)
    table_row = lax.broadcasted_iota(jnp.int32, table_ref.shape, 0)
    table_col = lax.broadcasted_iota(jnp.int32, table_ref.shape, 1)
    table_ref[...] = jnp.where(table_row == 0, -1, 0)
    count_ref[clusters] = 0
    source = lax.broadcasted_iota(jnp.int32, (rows, rows), 0)

    def work(step):
        load(step).wait()
        x = x_buf[pl.ds(pl.multiple_of(step * tall, tall), tall), :]
        order = order_ref[pl.ds(pl.multiple_of(step * STEP_BLOCKS, STEP_BLOCKS), STEP_BLOCKS), :]
        sketched = jnp.dot(x, sketch_ref[...], preferred_element_type=jnp.float32).astype(
            jnp.bfloat16
        )
        for i in range(STEP_BLOCKS):
            cluster = map_ref[step * STEP_BLOCKS + i]
            rank = count_ref[cluster]
            count_ref[cluster] = rank + 1
            block = sketched[i * rows : (i + 1) * rows]
            taken = jnp.where(source == order[i : i + 1, :], 1.0, 0.0).astype(jnp.bfloat16)
            slot = cluster * capacity + rank
            moved = dot_first(taken, block).astype(jnp.bfloat16)
            packed_buf[slot] = moved
            if spare:
                over = rank >= regular
                seen = count_ref[clusters]
                place = jnp.where(over, jnp.minimum(seen, spare), spare)
                count_ref[clusters] = seen + jnp.where(over, 1, 0)
                extra_ref[place] = moved
                here = (table_row == 0) & (table_col == place) & (place < spare)
                table_ref[...] = jnp.where(here, slot, table_ref[...])
            wide = jnp.concatenate([block, x[i * rows : (i + 1) * rows, :]], axis=1)
            sums_buf[cluster] += dot_first(block, wide)

    run(block_count // STEP_BLOCKS, work)
    excess = jnp.where(count_ref[clusters] > spare, 1, 0)
    table_ref[...] = jnp.where(table_row == 1, excess, table_ref[...])
    run(clusters, lambda c: store_sums(c).start())
    run(clusters, lambda c: store_packed(c).start())
    run(clusters, lambda c: store_sums(c).wait())
    run(clusters, lambda c: store_packed(c).wait())


def flip(index, mask):
    return index + mask - 2 * mask * lax.rem(lax.div(index, mask), 2)


def exchange_kernel(
    capacity,
    row_norm,
    leaves,
    lines,
    packed_ref,
    sums_ref,
    level_ref,
    extra_ref,
    table_ref,
    received_ref,
    inverse_ref,
    transfers_ref,
    summary_ref,
    extras_ref,
    tables_ref,
    excess_ref,
    *scratch,
):
    rounds = lines.bit_length() - 1
    halves = scratch[:rounds]
    partial = scratch[rounds : 2 * rounds]
    (
        landed,
        whole,
        nodes,
        siblings,
        block_send,
        block_recv,
        half_send,
        half_recv,
        leaf_send,
        leaf_recv,
        line_send,
        line_recv,
        node_send,
        node_recv,
        own_sem,
        excesses,
        table_send,
        table_recv,
        excess_send,
        excess_recv,
        extra_send,
        extra_recv,
    ) = scratch[2 * rounds :]
    regular, spare = shares_of(capacity)
    me = lax.axis_index("leaf")
    line = lax.axis_index("rows")
    rank = inverse_ref.shape[0]
    sample_cols = level_ref.shape[1]

    barrier = pltpu.get_barrier_semaphore()
    for d in range(1, leaves):
        pl.semaphore_signal(
            barrier, inc=1, device_id=(lax.rem(me + d, leaves), line), device_id_type=MESH
        )
    for d in range(1, lines):
        pl.semaphore_signal(
            barrier, inc=1, device_id=(me, lax.rem(line + d, lines)), device_id_type=MESH
        )
    pl.semaphore_wait(barrier, leaves + lines - 2)

    def remote(src, dst, send, recv, target):
        copy = pltpu.make_async_remote_copy(
            src_ref=src,
            dst_ref=dst,
            send_sem=send,
            recv_sem=recv,
            device_id=target,
            device_id_type=MESH,
        )
        copy.start()
        return copy

    pieces = max(1, regular // 4)
    depth = regular // pieces
    chunks = (leaves - 1) * pieces
    per = max(1, chunks // (5 + LEVELS + SPLITS * (LEVELS + 1)))
    after_sums = 3 * per
    first = chunks - per * (2 + LEVELS + SPLITS * LEVELS)

    def chunk(i):
        d = 1 + lax.rem(i, leaves - 1)
        offset = lax.div(i, leaves - 1) * depth
        peer = lax.rem(me + d, leaves)
        return pltpu.make_async_remote_copy(
            src_ref=packed_ref.at[pl.ds(peer * capacity + offset, depth)],
            dst_ref=received_ref.at[pl.ds(me * capacity + offset, depth)],
            send_sem=block_send.at[i],
            recv_sem=block_recv.at[i],
            device_id=(peer, line),
            device_id_type=MESH,
        )

    def send_chunks(base, count):
        run(count, lambda i: chunk(base + i).start())

    half = leaves // 2
    mirror = lax.rem(me + half, leaves)
    base_leaf = lax.div(me, half) * half
    others = [base_leaf + lax.rem(me - base_leaf + d, half) for d in range(1, half)]
    spares, tables = [], []
    if spare:
        stock = extra_ref.at[pl.ds(0, spare)]
        crossing = remote(
            stock, extras_ref.at[me], extra_send.at[0], extra_recv.at[0], (mirror, line)
        )
        for d, other in enumerate(others, 1):
            spares.append(
                remote(
                    stock, extras_ref.at[me], extra_send.at[d], extra_recv.at[d], (other, line)
                )
            )
        own_extra = pltpu.make_async_copy(stock, extras_ref.at[me], extra_send.at[2 * half])
        own_extra.start()
        tables_ref[me] = table_ref[...]
        for d in range(1, leaves):
            tables.append(
                remote(
                    table_ref,
                    tables_ref.at[me],
                    table_send.at[d],
                    table_recv.at[d],
                    (lax.rem(me + d, leaves), line),
                )
            )
    send_chunks(0, first)

    held, start, size = sums_ref, 0, rank
    for k in range(rounds):
        mask = 2**k
        size //= 2
        side = lax.rem(lax.div(line, mask), 2)
        copy = remote(
            held.at[:, pl.ds(pl.multiple_of((1 - side) * size, size), size), :],
            halves[k],
            half_send.at[k],
            half_recv.at[k],
            (me, flip(line, mask)),
        )
        if k == 0:
            own = pltpu.make_async_copy(
                packed_ref.at[pl.ds(me * capacity, regular)],
                received_ref.at[pl.ds(me * capacity, regular)],
                own_sem,
            )
            own.start()
        copy.wait()
        kept = pl.multiple_of(side * size, size)
        for c in range(leaves):
            partial[k][c] = held[c, pl.ds(kept, size), :] + halves[k][c]
        held, start = partial[k], start + side * size

    sums = []
    for d in range(1, leaves):
        peer = lax.rem(me + d, leaves)
        sums.append(
            remote(held.at[peer], landed.at[me], leaf_send.at[d], leaf_recv.at[d], (peer, line))
        )
    send_chunks(first, after_sums)
    total = held[me]
    for d in range(1, leaves):
        sums[d - 1].wait()
        total = total + landed[lax.rem(me - d + leaves, leaves)]
    start = pl.multiple_of(start, size)
    whole[pl.ds(start, size), :] = total
    shares = [
        remote(
            whole.at[pl.ds(start, size), :],
            whole.at[pl.ds(start, size), :],
            line_send.at[d],
            line_recv.at[d],
            (me, lax.rem(line + d, lines)),
        )
        for d in range(1, lines)
    ]
    for copy in shares:
        copy.wait()
    if spare:
        crossing.wait()
        for d, other in enumerate(others, 1):
            spares.append(
                remote(
                    extras_ref.at[mirror],
                    extras_ref.at[mirror],
                    extra_send.at[half + d],
                    extra_recv.at[half + d],
                    (other, line),
                )
            )

    eye = identity(rank)
    base = first + after_sums
    inverse = inverse_factor(
        whole[:, :rank] / row_norm + SHIFT * eye,
        lambda i, base=base: send_chunks(base + i * per, per),
    )
    base += SPLITS * per
    inverse_ref[...] = inverse
    nodes[0] = jnp.dot(inverse, whole[:, rank:], precision=HIGHEST) * (
        math.sqrt(sample_cols) / row_norm
    )
    for t in range(LEVELS):
        copy = remote(
            nodes.at[t], siblings.at[t], node_send.at[t], node_recv.at[t], (flip(me, 2**t), line)
        )
        busy = t < LEVELS - 1
        if busy:
            send_chunks(base, per)
            base += per
        own_node = nodes[t]
        sketch = level_ref[t]
        projected = jnp.dot(own_node, sketch, precision=HIGHEST)
        wide = jnp.concatenate([projected, own_node], axis=1)
        own_product = dot_first(projected, wide, HIGHEST)
        copy.wait()
        other_node = siblings[t]
        other = jnp.dot(other_node, sketch, precision=HIGHEST)
        other_wide = jnp.concatenate([other, other_node], axis=1)
        product = own_product + dot_first(other, other_wide, HIGHEST)
        inverse = inverse_factor(
            product[:, :rank] / (2 * rank) + SHIFT * eye,
            (lambda i, base=base: send_chunks(base + i * per, per)) if busy else None,
        )
        base += SPLITS * per
        transfers_ref[t] = dot_last(projected, inverse, HIGHEST)
        parent = jnp.dot(inverse, product[:, rank:], precision=HIGHEST) * (
            math.sqrt(sample_cols) / (2 * rank)
        )
        if t == LEVELS - 1:
            summary_ref[...] = parent
        else:
            nodes[t + 1] = parent

    if spare:
        for copy in tables:
            copy.wait()
        excess = tables_ref[0]
        for c in range(1, leaves):
            excess = jnp.maximum(excess, tables_ref[c])
        excesses[line] = excess
        flags = [
            remote(
                excesses.at[line],
                excesses.at[line],
                excess_send.at[d],
                excess_recv.at[d],
                (me, lax.rem(line + d, lines)),
            )
            for d in range(1, lines)
        ]
        for copy in flags:
            copy.wait()
        excess = excesses[0]
        for r in range(1, lines):
            excess = jnp.maximum(excess, excesses[r])
        excess_ref[...] = excess
        own_extra.wait()
        for copy in spares:
            copy.wait()
    else:
        tables_ref[...] = jnp.zeros(tables_ref.shape, jnp.int32)
        excess_ref[...] = jnp.zeros(excess_ref.shape, jnp.int32)
    own.wait()
    run(chunks, lambda i: chunk(i).wait())


def basis_kernel(rows_ref, inverse_ref, basis_ref, in_buf, out_buf, in_sem, out_sem):
    tall = rows_ref.shape[0] // BASIS_PARTS

    def span(i):
        return pl.ds(pl.multiple_of(i * tall, tall), tall)

    def load(i):
        return pltpu.make_async_copy(rows_ref.at[span(i)], in_buf.at[span(i)], in_sem.at[i])

    def store(i):
        return pltpu.make_async_copy(out_buf.at[span(i)], basis_ref.at[span(i)], out_sem.at[i])

    run(BASIS_PARTS, lambda i: load(i).start())
    inverse = inverse_ref[...]
    upper = inverse.astype(jnp.bfloat16)
    lower = (inverse - upper.astype(jnp.float32)).astype(jnp.bfloat16)
    both = jnp.concatenate([upper.T, lower.T], axis=0)

    def work(i):
        load(i).wait()
        rows = in_buf[span(i), :]
        twice = jnp.concatenate([rows, rows], axis=1)
        out_buf[span(i), :] = jnp.dot(twice, both, preferred_element_type=jnp.float32).astype(
            jnp.bfloat16
        )
        store(i).start()

    run(BASIS_PARTS, work)
    run(BASIS_PARTS, lambda i: store(i).wait())


def spread_kernel(
    capacity, tables_ref, rows_ref, extras_ref, inverse_ref, basis_ref, in_buf, out_buf,
    in_sem, extra_sem, out_sem,
):
    regular, spare = shares_of(capacity)
    me = lax.axis_index("leaf")
    leaves = rows_ref.shape[0] // capacity
    rows, rank = rows_ref.shape[1:]

    def load(c):
        span = pl.ds(c * capacity, regular)
        return pltpu.make_async_copy(rows_ref.at[span], in_buf.at[span], in_sem.at[c])

    def store(c):
        span = pl.ds(c * capacity, capacity)
        return pltpu.make_async_copy(out_buf.at[span], basis_ref.at[span], out_sem.at[c])

    def patch(c, e, act):
        slot = tables_ref[c, 0, e]

        @pl.when((slot >= me * capacity) & (slot < (me + 1) * capacity))
        def _():
            act(
                pltpu.make_async_copy(
                    extras_ref.at[c, e],
                    in_buf.at[c * capacity + slot - me * capacity],
                    extra_sem.at[c, e],
                )
            )

    run(leaves, lambda c: load(c).start())
    inverse = inverse_ref[...]
    upper = inverse.astype(jnp.bfloat16)
    lower = (inverse - upper.astype(jnp.float32)).astype(jnp.bfloat16)
    both = jnp.concatenate([upper.T, lower.T], axis=0)

    def begin(c):
        span = pl.ds(c * capacity + regular, capacity - regular)
        in_buf[span] = jnp.zeros((capacity - regular, rows, rank), jnp.bfloat16)
        for e in range(spare):
            patch(c, e, lambda copy: copy.start())

    run(leaves, begin)

    def work(c):
        load(c).wait()
        for e in range(spare):
            patch(c, e, lambda copy: copy.wait())
        blocks = in_buf[pl.ds(c * capacity, capacity)].reshape(capacity * rows, rank)
        twice = jnp.concatenate([blocks, blocks], axis=1)
        bases = jnp.dot(twice, both, preferred_element_type=jnp.float32).astype(jnp.bfloat16)
        out_buf[pl.ds(c * capacity, capacity)] = bases.reshape(capacity, rows, rank)
        store(c).start()

    run(leaves, work)
    run(leaves, lambda c: store(c).wait())


def body(samples, row_order, cluster_map, leaf_sketch, level_sketch):
    block_count = cluster_map.shape[0]
    block_rows = row_order.shape[1]
    sample_cols = samples.shape[1]
    rank = leaf_sketch.shape[1]
    leaves = lax.axis_size("leaf")
    lines = lax.axis_size("rows")
    capacity = 2 * block_count // leaves
    slots = leaves * capacity
    width = rank + sample_cols
    row_norm = float(lines * block_count * block_rows)
    vmem = pl.BlockSpec(memory_space=pltpu.VMEM)
    anywhere = pl.BlockSpec(memory_space=pl.ANY)
    dma = pltpu.SemaphoreType.DMA

    regular, spare = shares_of(capacity)
    table = jax.ShapeDtypeStruct((8, 128), jnp.int32)
    packed, sums, extra, own_table = pl.pallas_call(
        functools.partial(local_kernel, capacity),
        in_specs=[pl.BlockSpec(memory_space=pltpu.SMEM), vmem, anywhere, vmem],
        out_specs=[anywhere, anywhere, vmem, vmem],
        out_shape=[
            jax.ShapeDtypeStruct((slots, block_rows, rank), jnp.bfloat16),
            jax.ShapeDtypeStruct((leaves, rank, width), jnp.float32),
            jax.ShapeDtypeStruct((spare + 1, block_rows, rank), jnp.bfloat16),
            table,
        ],
        scratch_shapes=[
            pltpu.VMEM((block_count * block_rows, sample_cols), jnp.bfloat16),
            pltpu.VMEM((slots, block_rows, rank), jnp.bfloat16),
            pltpu.VMEM((leaves, rank, width), jnp.float32),
            pltpu.SMEM((leaves + 1,), jnp.int32),
            dma((block_count // STEP_BLOCKS,)),
            dma((leaves,)),
            dma((leaves,)),
        ],
        compiler_params=pltpu.CompilerParams(vmem_limit_bytes=VMEM_BYTES),
        name="sketch_blocks",
    )(cluster_map, row_order, samples, leaf_sketch)

    rounds = lines.bit_length() - 1
    shares = [
        pltpu.VMEM((leaves, rank >> (k + 1), width), jnp.float32) for k in range(rounds)
    ]
    chunks = (leaves - 1) * max(1, regular // 4)
    received, inverse, transfers, summary, extras, tables, excess = pl.pallas_call(
        functools.partial(exchange_kernel, capacity, row_norm, leaves, lines),
        in_specs=[anywhere, vmem, vmem, anywhere, vmem],
        out_specs=[anywhere, vmem, vmem, vmem, anywhere, vmem, vmem],
        out_shape=[
            jax.ShapeDtypeStruct((slots, block_rows, rank), jnp.bfloat16),
            jax.ShapeDtypeStruct((rank, rank), jnp.float32),
            jax.ShapeDtypeStruct((LEVELS, rank, rank), jnp.float32),
            jax.ShapeDtypeStruct((rank, sample_cols), jnp.float32),
            jax.ShapeDtypeStruct((leaves, max(spare, 1), block_rows, rank), jnp.bfloat16),
            jax.ShapeDtypeStruct((leaves, 8, 128), jnp.int32),
            table,
        ],
        scratch_shapes=[
            *shares,
            *shares,
            pltpu.VMEM((leaves, rank // lines, width), jnp.float32),
            pltpu.VMEM((rank, width), jnp.float32),
            pltpu.VMEM((LEVELS, rank, sample_cols), jnp.float32),
            pltpu.VMEM((LEVELS, rank, sample_cols), jnp.float32),
            dma((chunks,)),
            dma((chunks,)),
            dma((rounds,)),
            dma((rounds,)),
            dma((leaves,)),
            dma((leaves,)),
            dma((lines,)),
            dma((lines,)),
            dma((LEVELS,)),
            dma((LEVELS,)),
            dma,
            pltpu.VMEM((lines, 8, 128), jnp.int32),
            dma((leaves,)),
            dma((leaves,)),
            dma((lines,)),
            dma((lines,)),
            dma((leaves + 1,)),
            dma((leaves + 1,)),
        ],
        compiler_params=pltpu.CompilerParams(
            collective_id=0, has_side_effects=True, vmem_limit_bytes=VMEM_BYTES
        ),
        name="exchange_and_merge",
    )(packed, sums, level_sketch, extra, own_table)

    total_rows = slots * block_rows

    def all_slots(full):
        return pl.pallas_call(
            basis_kernel,
            in_specs=[anywhere, vmem],
            out_specs=anywhere,
            out_shape=jax.ShapeDtypeStruct((total_rows, rank), jnp.bfloat16),
            scratch_shapes=[
                pltpu.VMEM((total_rows, rank), jnp.bfloat16),
                pltpu.VMEM((total_rows, rank), jnp.bfloat16),
                dma((BASIS_PARTS,)),
                dma((BASIS_PARTS,)),
            ],
            compiler_params=pltpu.CompilerParams(vmem_limit_bytes=VMEM_BYTES),
            name="leaf_bases",
        )(full.reshape(total_rows, rank), inverse)

    def send_again():
        return all_slots(lax.all_to_all(packed, "leaf", split_axis=0, concat_axis=0, tiled=True))

    def spread():
        return pl.pallas_call(
            functools.partial(spread_kernel, capacity),
            in_specs=[pl.BlockSpec(memory_space=pltpu.SMEM), anywhere, anywhere, vmem],
            out_specs=anywhere,
            out_shape=jax.ShapeDtypeStruct((slots, block_rows, rank), jnp.bfloat16),
            scratch_shapes=[
                pltpu.VMEM((slots, block_rows, rank), jnp.bfloat16),
                pltpu.VMEM((slots, block_rows, rank), jnp.bfloat16),
                dma((leaves,)),
                dma((leaves, spare)),
                dma((leaves,)),
            ],
            compiler_params=pltpu.CompilerParams(vmem_limit_bytes=VMEM_BYTES),
            name="spread_bases",
        )(tables, received, extras, inverse).reshape(total_rows, rank)

    if spare:
        basis = lax.cond(excess[1, 0] > 0, send_again, spread)
    else:
        basis = all_slots(received)
    return basis, transfers[None], summary[None]


def solution(mesh):
    in_specs = (P(("leaf", "rows"), None), P(("leaf", "rows"), None), P(("leaf", "rows")), P(), P())
    out_specs = (P(("leaf", "rows"), None), P("leaf", None, None, None), P("leaf", None, None))
    return jax.shard_map(body, mesh=mesh, in_specs=in_specs, out_specs=out_specs, check_vma=False)
```

```python
import functools
import math

import jax
import jax.numpy as jnp
from jax import lax
from jax.experimental import pallas as pl
from jax.experimental.pallas import tpu as pltpu
from jax.sharding import PartitionSpec as P

LEVELS = 3
SHIFT = 0.01
TILE = 8
SPLITS = 4
STEP_BLOCKS = 8
BASIS_PARTS = 16
VMEM_BYTES = 56 * 1024 * 1024
MESH = pl.DeviceIdType.MESH
HIGHEST = lax.Precision.HIGHEST


def dot_first(left, right, precision=None):
    return lax.dot_general(
        left,
        right,
        (((0,), (0,)), ((), ())),
        precision=precision,
        preferred_element_type=jnp.float32,
    )


def dot_last(left, right, precision=None):
    return lax.dot_general(
        left,
        right,
        (((1,), (1,)), ((), ())),
        precision=precision,
        preferred_element_type=jnp.float32,
    )


def identity(size):
    rows = lax.broadcasted_iota(jnp.int32, (size, size), 0)
    cols = lax.broadcasted_iota(jnp.int32, (size, size), 1)
    return jnp.where(rows == cols, 1.0, 0.0).astype(jnp.float32)


def inverse_factor(gram, between=None):
    size = gram.shape[0]
    part_rows = size // SPLITS
    row_id = lax.broadcasted_iota(jnp.int32, (TILE, size), 0)
    col_id = lax.broadcasted_iota(jnp.int32, (TILE, size), 1)
    one_row = lax.broadcasted_iota(jnp.int32, (1, size), 1)
    done = []
    m = gram
    for part in range(SPLITS):
        if between is not None:
            between(part)
        live = size - part * part_rows
        group = 2 if live > 96 else 4
        keep_cols = lax.broadcasted_iota(jnp.int32, (live, size), 1)

        def panel(i, m, part=part, live=live, group=group, keep_cols=keep_cols):
            first = jnp.zeros((TILE, size), jnp.float32)
            for s in range(0, TILE, group):
                cols = [
                    jnp.broadcast_to(m[:, s + j : s + j + 1], (live, size)) for j in range(group)
                ]
                inside = (one_row >= s) & (one_row < s + group)
                rows = [
                    jnp.where(inside, jnp.where(one_row == s + j, 1.0, 0.0), m[s + j : s + j + 1])
                    for j in range(group)
                ]
                m = jnp.where((keep_cols >= s) & (keep_cols < s + group), 0.0, m)
                for j in range(group):
                    scale = lax.rsqrt(cols[j][s + j : s + j + 1, :])
                    inv = scale * scale
                    for k in range(j + 1, group):
                        factor = cols[j][s + k : s + k + 1, :] * inv
                        cols[k] = cols[k] - cols[j] * factor
                        rows[k] = rows[k] - factor * rows[j]
                    top = jnp.where(row_id > s + j, cols[j][:TILE], 0.0)
                    below = jnp.concatenate([top, cols[j][TILE:]], axis=0)
                    m = m - below * (rows[j] * inv)
                    first = jnp.where(row_id == s + j, rows[j] * scale, first)
            unused = size - TILE * (part * (part_rows // TILE) + i)
            first = jnp.where((col_id > row_id) & (col_id < unused), 0.0, first)
            m = jnp.concatenate([m[TILE:], first], axis=0)
            return pltpu.roll(m, size - TILE, 1)

        m = lax.fori_loop(0, part_rows // TILE, panel, m)
        finished = m[live - part_rows :]
        turned = (part + 1) * part_rows
        done.append(pltpu.roll(finished, turned, 1) if turned < size else finished)
        m = m[: live - part_rows]
    return jnp.concatenate(done, axis=0)


def shares_of(capacity):
    if capacity % 16:
        return capacity, 0
    return 3 * capacity // 4, 3 * capacity // 8


def run(count, work):
    def one(i, carry):
        work(i)
        return carry

    lax.fori_loop(0, count, one, 0)


def local_kernel(
    capacity,
    map_ref,
    order_ref,
    x_ref,
    sketch_ref,
    packed_ref,
    sums_ref,
    extra_ref,
    table_ref,
    x_buf,
    packed_buf,
    sums_buf,
    count_ref,
    in_sem,
    packed_sem,
    sums_sem,
):
    regular, spare = shares_of(capacity)
    clusters = sums_ref.shape[0]
    block_count, rows = order_ref.shape
    tall = STEP_BLOCKS * rows

    def load(step):
        span = pl.ds(pl.multiple_of(step * tall, tall), tall)
        return pltpu.make_async_copy(x_ref.at[span], x_buf.at[span], in_sem.at[step])

    def store_packed(c):
        span = pl.ds(c * capacity, capacity)
        return pltpu.make_async_copy(packed_buf.at[span], packed_ref.at[span], packed_sem.at[c])

    def store_sums(c):
        return pltpu.make_async_copy(sums_buf.at[c], sums_ref.at[c], sums_sem.at[c])

    def clear(c):
        count_ref[c] = 0
        sums_buf[c] = jnp.zeros(sums_buf.shape[1:], jnp.float32)
        for j in range(capacity):
            packed_buf[c * capacity + j] = jnp.zeros(packed_buf.shape[1:], jnp.bfloat16)

    run(block_count // STEP_BLOCKS, lambda step: load(step).start())
    run(clusters, clear)
    extra_ref[...] = jnp.zeros(extra_ref.shape, jnp.bfloat16)
    table_row = lax.broadcasted_iota(jnp.int32, table_ref.shape, 0)
    table_col = lax.broadcasted_iota(jnp.int32, table_ref.shape, 1)
    table_ref[...] = jnp.where(table_row == 0, -1, 0)
    count_ref[clusters] = 0
    source = lax.broadcasted_iota(jnp.int32, (rows, rows), 0)

    def work(step):
        load(step).wait()
        x = x_buf[pl.ds(pl.multiple_of(step * tall, tall), tall), :]
        order = order_ref[pl.ds(pl.multiple_of(step * STEP_BLOCKS, STEP_BLOCKS), STEP_BLOCKS), :]
        sketched = jnp.dot(x, sketch_ref[...], preferred_element_type=jnp.float32).astype(
            jnp.bfloat16
        )
        for i in range(STEP_BLOCKS):
            cluster = map_ref[step * STEP_BLOCKS + i]
            rank = count_ref[cluster]
            count_ref[cluster] = rank + 1
            block = sketched[i * rows : (i + 1) * rows]
            taken = jnp.where(source == order[i : i + 1, :], 1.0, 0.0).astype(jnp.bfloat16)
            slot = cluster * capacity + rank
            moved = dot_first(taken, block).astype(jnp.bfloat16)
            packed_buf[slot] = moved
            if spare:
                over = rank >= regular
                seen = count_ref[clusters]
                place = jnp.where(over, jnp.minimum(seen, spare), spare)
                count_ref[clusters] = seen + jnp.where(over, 1, 0)
                extra_ref[place] = moved
                here = (table_row == 0) & (table_col == place) & (place < spare)
                table_ref[...] = jnp.where(here, slot, table_ref[...])
            wide = jnp.concatenate([block, x[i * rows : (i + 1) * rows, :]], axis=1)
            sums_buf[cluster] += dot_first(block, wide)

    run(block_count // STEP_BLOCKS, work)
    excess = jnp.where(count_ref[clusters] > spare, 1, 0)
    table_ref[...] = jnp.where(table_row == 1, excess, table_ref[...])
    run(clusters, lambda c: store_sums(c).start())
    run(clusters, lambda c: store_packed(c).start())
    run(clusters, lambda c: store_sums(c).wait())
    run(clusters, lambda c: store_packed(c).wait())


def flip(index, mask):
    return index + mask - 2 * mask * lax.rem(lax.div(index, mask), 2)


def exchange_kernel(
    capacity,
    row_norm,
    leaves,
    lines,
    packed_ref,
    sums_ref,
    level_ref,
    extra_ref,
    table_ref,
    received_ref,
    inverse_ref,
    transfers_ref,
    summary_ref,
    extras_ref,
    tables_ref,
    excess_ref,
    *scratch,
):
    rounds = lines.bit_length() - 1
    halves = scratch[:rounds]
    partial = scratch[rounds : 2 * rounds]
    (
        landed,
        whole,
        nodes,
        siblings,
        block_send,
        block_recv,
        half_send,
        half_recv,
        leaf_send,
        leaf_recv,
        line_send,
        line_recv,
        node_send,
        node_recv,
        own_sem,
        excesses,
        table_send,
        table_recv,
        excess_send,
        excess_recv,
        extra_send,
        extra_recv,
    ) = scratch[2 * rounds :]
    regular, spare = shares_of(capacity)
    me = lax.axis_index("leaf")
    line = lax.axis_index("rows")
    rank = inverse_ref.shape[0]
    sample_cols = level_ref.shape[1]

    barrier = pltpu.get_barrier_semaphore()
    for d in range(1, leaves):
        pl.semaphore_signal(
            barrier, inc=1, device_id=(lax.rem(me + d, leaves), line), device_id_type=MESH
        )
    for d in range(1, lines):
        pl.semaphore_signal(
            barrier, inc=1, device_id=(me, lax.rem(line + d, lines)), device_id_type=MESH
        )
    pl.semaphore_wait(barrier, leaves + lines - 2)

    def remote(src, dst, send, recv, target):
        copy = pltpu.make_async_remote_copy(
            src_ref=src,
            dst_ref=dst,
            send_sem=send,
            recv_sem=recv,
            device_id=target,
            device_id_type=MESH,
        )
        copy.start()
        return copy

    pieces = max(1, regular // 4)
    depth = regular // pieces
    chunks = (leaves - 1) * pieces
    per = max(1, chunks // (5 + LEVELS + SPLITS * (LEVELS + 1)))
    after_sums = 3 * per
    first = chunks - per * (2 + LEVELS + SPLITS * LEVELS)

    def chunk(i):
        d = 1 + lax.rem(i, leaves - 1)
        offset = lax.div(i, leaves - 1) * depth
        peer = lax.rem(me + d, leaves)
        return pltpu.make_async_remote_copy(
            src_ref=packed_ref.at[pl.ds(peer * capacity + offset, depth)],
            dst_ref=received_ref.at[pl.ds(me * capacity + offset, depth)],
            send_sem=block_send.at[i],
            recv_sem=block_recv.at[i],
            device_id=(peer, line),
            device_id_type=MESH,
        )

    def send_chunks(base, count):
        run(count, lambda i: chunk(base + i).start())

    half = leaves // 2
    mirror = lax.rem(me + half, leaves)
    base_leaf = lax.div(me, half) * half
    others = [base_leaf + lax.rem(me - base_leaf + d, half) for d in range(1, half)]
    spares, tables = [], []
    if spare:
        stock = extra_ref.at[pl.ds(0, spare)]
        crossing = remote(
            stock, extras_ref.at[me], extra_send.at[0], extra_recv.at[0], (mirror, line)
        )
        for d, other in enumerate(others, 1):
            spares.append(
                remote(
                    stock, extras_ref.at[me], extra_send.at[d], extra_recv.at[d], (other, line)
                )
            )
        own_extra = pltpu.make_async_copy(stock, extras_ref.at[me], extra_send.at[2 * half])
        own_extra.start()
        tables_ref[me] = table_ref[...]
        for d in range(1, leaves):
            tables.append(
                remote(
                    table_ref,
                    tables_ref.at[me],
                    table_send.at[d],
                    table_recv.at[d],
                    (lax.rem(me + d, leaves), line),
                )
            )
    send_chunks(0, first)

    held, start, size = sums_ref, 0, rank
    for k in range(rounds):
        mask = 2**k
        size //= 2
        side = lax.rem(lax.div(line, mask), 2)
        copy = remote(
            held.at[:, pl.ds(pl.multiple_of((1 - side) * size, size), size), :],
            halves[k],
            half_send.at[k],
            half_recv.at[k],
            (me, flip(line, mask)),
        )
        if k == 0:
            own = pltpu.make_async_copy(
                packed_ref.at[pl.ds(me * capacity, regular)],
                received_ref.at[pl.ds(me * capacity, regular)],
                own_sem,
            )
            own.start()
        copy.wait()
        kept = pl.multiple_of(side * size, size)
        for c in range(leaves):
            partial[k][c] = held[c, pl.ds(kept, size), :] + halves[k][c]
        held, start = partial[k], start + side * size

    sums = []
    for d in range(1, leaves):
        peer = lax.rem(me + d, leaves)
        sums.append(
            remote(held.at[peer], landed.at[me], leaf_send.at[d], leaf_recv.at[d], (peer, line))
        )
    send_chunks(first, after_sums)
    total = held[me]
    for d in range(1, leaves):
        sums[d - 1].wait()
        total = total + landed[lax.rem(me - d + leaves, leaves)]
    start = pl.multiple_of(start, size)
    whole[pl.ds(start, size), :] = total
    shares = [
        remote(
            whole.at[pl.ds(start, size), :],
            whole.at[pl.ds(start, size), :],
            line_send.at[d],
            line_recv.at[d],
            (me, lax.rem(line + d, lines)),
        )
        for d in range(1, lines)
    ]
    for copy in shares:
        copy.wait()
    if spare:
        crossing.wait()
        for d, other in enumerate(others, 1):
            spares.append(
                remote(
                    extras_ref.at[mirror],
                    extras_ref.at[mirror],
                    extra_send.at[half + d],
                    extra_recv.at[half + d],
                    (other, line),
                )
            )

    eye = identity(rank)
    base = first + after_sums
    inverse = inverse_factor(
        whole[:, :rank] / row_norm + SHIFT * eye,
        lambda i, base=base: send_chunks(base + i * per, per),
    )
    base += SPLITS * per
    inverse_ref[...] = inverse
    nodes[0] = jnp.dot(inverse, whole[:, rank:], precision=HIGHEST) * (
        math.sqrt(sample_cols) / row_norm
    )
    for t in range(LEVELS):
        copy = remote(
            nodes.at[t], siblings.at[t], node_send.at[t], node_recv.at[t], (flip(me, 2**t), line)
        )
        busy = t < LEVELS - 1
        if busy:
            send_chunks(base, per)
            base += per
        own_node = nodes[t]
        sketch = level_ref[t]
        projected = jnp.dot(own_node, sketch, precision=HIGHEST)
        wide = jnp.concatenate([projected, own_node], axis=1)
        own_product = dot_first(projected, wide, HIGHEST)
        copy.wait()
        other_node = siblings[t]
        other = jnp.dot(other_node, sketch, precision=HIGHEST)
        other_wide = jnp.concatenate([other, other_node], axis=1)
        product = own_product + dot_first(other, other_wide, HIGHEST)
        inverse = inverse_factor(
            product[:, :rank] / (2 * rank) + SHIFT * eye,
            (lambda i, base=base: send_chunks(base + i * per, per)) if busy else None,
        )
        base += SPLITS * per
        transfers_ref[t] = dot_last(projected, inverse, HIGHEST)
        parent = jnp.dot(inverse, product[:, rank:], precision=HIGHEST) * (
            math.sqrt(sample_cols) / (2 * rank)
        )
        if t == LEVELS - 1:
            summary_ref[...] = parent
        else:
            nodes[t + 1] = parent

    if spare:
        for copy in tables:
            copy.wait()
        excess = tables_ref[0]
        for c in range(1, leaves):
            excess = jnp.maximum(excess, tables_ref[c])
        excesses[line] = excess
        flags = [
            remote(
                excesses.at[line],
                excesses.at[line],
                excess_send.at[d],
                excess_recv.at[d],
                (me, lax.rem(line + d, lines)),
            )
            for d in range(1, lines)
        ]
        for copy in flags:
            copy.wait()
        excess = excesses[0]
        for r in range(1, lines):
            excess = jnp.maximum(excess, excesses[r])
        excess_ref[...] = excess
        own_extra.wait()
        for copy in spares:
            copy.wait()
    else:
        tables_ref[...] = jnp.zeros(tables_ref.shape, jnp.int32)
        excess_ref[...] = jnp.zeros(excess_ref.shape, jnp.int32)
    own.wait()
    run(chunks, lambda i: chunk(i).wait())


def basis_kernel(rows_ref, inverse_ref, basis_ref, in_buf, out_buf, in_sem, out_sem):
    tall = rows_ref.shape[0] // BASIS_PARTS

    def span(i):
        return pl.ds(pl.multiple_of(i * tall, tall), tall)

    def load(i):
        return pltpu.make_async_copy(rows_ref.at[span(i)], in_buf.at[span(i)], in_sem.at[i])

    def store(i):
        return pltpu.make_async_copy(out_buf.at[span(i)], basis_ref.at[span(i)], out_sem.at[i])

    run(BASIS_PARTS, lambda i: load(i).start())
    inverse = inverse_ref[...]
    upper = inverse.astype(jnp.bfloat16)
    lower = (inverse - upper.astype(jnp.float32)).astype(jnp.bfloat16)
    both = jnp.concatenate([upper.T, lower.T], axis=0)

    def work(i):
        load(i).wait()
        rows = in_buf[span(i), :]
        twice = jnp.concatenate([rows, rows], axis=1)
        out_buf[span(i), :] = jnp.dot(twice, both, preferred_element_type=jnp.float32).astype(
            jnp.bfloat16
        )
        store(i).start()

    run(BASIS_PARTS, work)
    run(BASIS_PARTS, lambda i: store(i).wait())


def spread_kernel(
    capacity, tables_ref, rows_ref, extras_ref, inverse_ref, basis_ref, in_buf, out_buf,
    in_sem, extra_sem, out_sem,
):
    regular, spare = shares_of(capacity)
    me = lax.axis_index("leaf")
    leaves = rows_ref.shape[0] // capacity
    rows, rank = rows_ref.shape[1:]

    def load(c):
        span = pl.ds(c * capacity, regular)
        return pltpu.make_async_copy(rows_ref.at[span], in_buf.at[span], in_sem.at[c])

    def store(c):
        span = pl.ds(c * capacity, capacity)
        return pltpu.make_async_copy(out_buf.at[span], basis_ref.at[span], out_sem.at[c])

    def patch(c, e, act):
        slot = tables_ref[c, 0, e]

        @pl.when((slot >= me * capacity) & (slot < (me + 1) * capacity))
        def _():
            act(
                pltpu.make_async_copy(
                    extras_ref.at[c, e],
                    in_buf.at[c * capacity + slot - me * capacity],
                    extra_sem.at[c, e],
                )
            )

    run(leaves, lambda c: load(c).start())
    inverse = inverse_ref[...]
    upper = inverse.astype(jnp.bfloat16)
    lower = (inverse - upper.astype(jnp.float32)).astype(jnp.bfloat16)
    both = jnp.concatenate([upper.T, lower.T], axis=0)

    def begin(c):
        span = pl.ds(c * capacity + regular, capacity - regular)
        in_buf[span] = jnp.zeros((capacity - regular, rows, rank), jnp.bfloat16)
        for e in range(spare):
            patch(c, e, lambda copy: copy.start())

    run(leaves, begin)

    def work(c):
        load(c).wait()
        for e in range(spare):
            patch(c, e, lambda copy: copy.wait())
        blocks = in_buf[pl.ds(c * capacity, capacity)].reshape(capacity * rows, rank)
        twice = jnp.concatenate([blocks, blocks], axis=1)
        bases = jnp.dot(twice, both, preferred_element_type=jnp.float32).astype(jnp.bfloat16)
        out_buf[pl.ds(c * capacity, capacity)] = bases.reshape(capacity, rows, rank)
        store(c).start()

    run(leaves, work)
    run(leaves, lambda c: store(c).wait())


def body(samples, row_order, cluster_map, leaf_sketch, level_sketch):
    block_count = cluster_map.shape[0]
    block_rows = row_order.shape[1]
    sample_cols = samples.shape[1]
    rank = leaf_sketch.shape[1]
    leaves = lax.axis_size("leaf")
    lines = lax.axis_size("rows")
    capacity = 2 * block_count // leaves
    slots = leaves * capacity
    width = rank + sample_cols
    row_norm = float(lines * block_count * block_rows)
    vmem = pl.BlockSpec(memory_space=pltpu.VMEM)
    anywhere = pl.BlockSpec(memory_space=pl.ANY)
    dma = pltpu.SemaphoreType.DMA

    regular, spare = shares_of(capacity)
    table = jax.ShapeDtypeStruct((8, 128), jnp.int32)
    packed, sums, extra, own_table = pl.pallas_call(
        functools.partial(local_kernel, capacity),
        in_specs=[pl.BlockSpec(memory_space=pltpu.SMEM), vmem, anywhere, vmem],
        out_specs=[anywhere, anywhere, vmem, vmem],
        out_shape=[
            jax.ShapeDtypeStruct((slots, block_rows, rank), jnp.bfloat16),
            jax.ShapeDtypeStruct((leaves, rank, width), jnp.float32),
            jax.ShapeDtypeStruct((spare + 1, block_rows, rank), jnp.bfloat16),
            table,
        ],
        scratch_shapes=[
            pltpu.VMEM((block_count * block_rows, sample_cols), jnp.bfloat16),
            pltpu.VMEM((slots, block_rows, rank), jnp.bfloat16),
            pltpu.VMEM((leaves, rank, width), jnp.float32),
            pltpu.SMEM((leaves + 1,), jnp.int32),
            dma((block_count // STEP_BLOCKS,)),
            dma((leaves,)),
            dma((leaves,)),
        ],
        compiler_params=pltpu.CompilerParams(vmem_limit_bytes=VMEM_BYTES),
        name="sketch_blocks",
    )(cluster_map, row_order, samples, leaf_sketch)

    rounds = lines.bit_length() - 1
    shares = [
        pltpu.VMEM((leaves, rank >> (k + 1), width), jnp.float32) for k in range(rounds)
    ]
    chunks = (leaves - 1) * max(1, regular // 4)
    received, inverse, transfers, summary, extras, tables, excess = pl.pallas_call(
        functools.partial(exchange_kernel, capacity, row_norm, leaves, lines),
        in_specs=[anywhere, vmem, vmem, anywhere, vmem],
        out_specs=[anywhere, vmem, vmem, vmem, anywhere, vmem, vmem],
        out_shape=[
            jax.ShapeDtypeStruct((slots, block_rows, rank), jnp.bfloat16),
            jax.ShapeDtypeStruct((rank, rank), jnp.float32),
            jax.ShapeDtypeStruct((LEVELS, rank, rank), jnp.float32),
            jax.ShapeDtypeStruct((rank, sample_cols), jnp.float32),
            jax.ShapeDtypeStruct((leaves, max(spare, 1), block_rows, rank), jnp.bfloat16),
            jax.ShapeDtypeStruct((leaves, 8, 128), jnp.int32),
            table,
        ],
        scratch_shapes=[
            *shares,
            *shares,
            pltpu.VMEM((leaves, rank // lines, width), jnp.float32),
            pltpu.VMEM((rank, width), jnp.float32),
            pltpu.VMEM((LEVELS, rank, sample_cols), jnp.float32),
            pltpu.VMEM((LEVELS, rank, sample_cols), jnp.float32),
            dma((chunks,)),
            dma((chunks,)),
            dma((rounds,)),
            dma((rounds,)),
            dma((leaves,)),
            dma((leaves,)),
            dma((lines,)),
            dma((lines,)),
            dma((LEVELS,)),
            dma((LEVELS,)),
            dma,
            pltpu.VMEM((lines, 8, 128), jnp.int32),
            dma((leaves,)),
            dma((leaves,)),
            dma((lines,)),
            dma((lines,)),
            dma((leaves + 1,)),
            dma((leaves + 1,)),
        ],
        compiler_params=pltpu.CompilerParams(
            collective_id=0, has_side_effects=True, vmem_limit_bytes=VMEM_BYTES
        ),
        name="exchange_and_merge",
    )(packed, sums, level_sketch, extra, own_table)

    total_rows = slots * block_rows

    def all_slots(full):
        return pl.pallas_call(
            basis_kernel,
            in_specs=[anywhere, vmem],
            out_specs=anywhere,
            out_shape=jax.ShapeDtypeStruct((total_rows, rank), jnp.bfloat16),
            scratch_shapes=[
                pltpu.VMEM((total_rows, rank), jnp.bfloat16),
                pltpu.VMEM((total_rows, rank), jnp.bfloat16),
                dma((BASIS_PARTS,)),
                dma((BASIS_PARTS,)),
            ],
            compiler_params=pltpu.CompilerParams(vmem_limit_bytes=VMEM_BYTES),
            name="leaf_bases",
        )(full.reshape(total_rows, rank), inverse)

    def send_again():
        return all_slots(lax.all_to_all(packed, "leaf", split_axis=0, concat_axis=0, tiled=True))

    def spread():
        return pl.pallas_call(
            functools.partial(spread_kernel, capacity),
            in_specs=[pl.BlockSpec(memory_space=pltpu.SMEM), anywhere, anywhere, vmem],
            out_specs=anywhere,
            out_shape=jax.ShapeDtypeStruct((slots, block_rows, rank), jnp.bfloat16),
            scratch_shapes=[
                pltpu.VMEM((slots, block_rows, rank), jnp.bfloat16),
                pltpu.VMEM((slots, block_rows, rank), jnp.bfloat16),
                dma((leaves,)),
                dma((leaves, spare)),
                dma((leaves,)),
            ],
            compiler_params=pltpu.CompilerParams(vmem_limit_bytes=VMEM_BYTES),
            name="spread_bases",
        )(tables, received, extras, inverse).reshape(total_rows, rank)

    if spare:
        basis = lax.cond(excess[1, 0] > 0, send_again, spread)
    else:
        basis = all_slots(received)
    return basis, transfers[None], summary[None]


def solution(mesh):
    in_specs = (P(("leaf", "rows"), None), P(("leaf", "rows"), None), P(("leaf", "rows")), P(), P())
    out_specs = (P(("leaf", "rows"), None), P("leaf", None, None, None), P("leaf", None, None))
    return jax.shard_map(body, mesh=mesh, in_specs=in_specs, out_specs=out_specs, check_vma=False)
```

```python
import functools
import math

import jax
import jax.numpy as jnp
from jax import lax
from jax.experimental import pallas as pl
from jax.experimental.pallas import tpu as pltpu
from jax.sharding import PartitionSpec as P

LEVELS = 3
SHIFT = 0.01
TILE = 8
SPLITS = 4
STEP_BLOCKS = 8
BASIS_PARTS = 16
VMEM_BYTES = 56 * 1024 * 1024
MESH = pl.DeviceIdType.MESH
HIGHEST = lax.Precision.HIGHEST


def dot_first(left, right, precision=None):
    return lax.dot_general(
        left,
        right,
        (((0,), (0,)), ((), ())),
        precision=precision,
        preferred_element_type=jnp.float32,
    )


def dot_last(left, right, precision=None):
    return lax.dot_general(
        left,
        right,
        (((1,), (1,)), ((), ())),
        precision=precision,
        preferred_element_type=jnp.float32,
    )


def identity(size):
    rows = lax.broadcasted_iota(jnp.int32, (size, size), 0)
    cols = lax.broadcasted_iota(jnp.int32, (size, size), 1)
    return jnp.where(rows == cols, 1.0, 0.0).astype(jnp.float32)


def inverse_factor(gram, between=None):
    size = gram.shape[0]
    part_rows = size // SPLITS
    row_id = lax.broadcasted_iota(jnp.int32, (TILE, size), 0)
    col_id = lax.broadcasted_iota(jnp.int32, (TILE, size), 1)
    one_row = lax.broadcasted_iota(jnp.int32, (1, size), 1)
    done = []
    m = gram
    for part in range(SPLITS):
        if between is not None:
            between(part)
        live = size - part * part_rows
        group = 2 if live > 96 else 4
        keep_cols = lax.broadcasted_iota(jnp.int32, (live, size), 1)

        def panel(i, m, part=part, live=live, group=group, keep_cols=keep_cols):
            first = jnp.zeros((TILE, size), jnp.float32)
            for s in range(0, TILE, group):
                cols = [
                    jnp.broadcast_to(m[:, s + j : s + j + 1], (live, size)) for j in range(group)
                ]
                inside = (one_row >= s) & (one_row < s + group)
                rows = [
                    jnp.where(inside, jnp.where(one_row == s + j, 1.0, 0.0), m[s + j : s + j + 1])
                    for j in range(group)
                ]
                m = jnp.where((keep_cols >= s) & (keep_cols < s + group), 0.0, m)
                for j in range(group):
                    scale = lax.rsqrt(cols[j][s + j : s + j + 1, :])
                    inv = scale * scale
                    for k in range(j + 1, group):
                        factor = cols[j][s + k : s + k + 1, :] * inv
                        cols[k] = cols[k] - cols[j] * factor
                        rows[k] = rows[k] - factor * rows[j]
                    top = jnp.where(row_id > s + j, cols[j][:TILE], 0.0)
                    below = jnp.concatenate([top, cols[j][TILE:]], axis=0)
                    m = m - below * (rows[j] * inv)
                    first = jnp.where(row_id == s + j, rows[j] * scale, first)
            unused = size - TILE * (part * (part_rows // TILE) + i)
            first = jnp.where((col_id > row_id) & (col_id < unused), 0.0, first)
            m = jnp.concatenate([m[TILE:], first], axis=0)
            return pltpu.roll(m, size - TILE, 1)

        m = lax.fori_loop(0, part_rows // TILE, panel, m)
        finished = m[live - part_rows :]
        turned = (part + 1) * part_rows
        done.append(pltpu.roll(finished, turned, 1) if turned < size else finished)
        m = m[: live - part_rows]
    return jnp.concatenate(done, axis=0)


def shares_of(capacity):
    if capacity % 16:
        return capacity, 0
    return 3 * capacity // 4, 3 * capacity // 8


def run(count, work):
    def one(i, carry):
        work(i)
        return carry

    lax.fori_loop(0, count, one, 0)


def local_kernel(
    capacity,
    map_ref,
    order_ref,
    x_ref,
    sketch_ref,
    packed_ref,
    sums_ref,
    extra_ref,
    table_ref,
    x_buf,
    packed_buf,
    sums_buf,
    count_ref,
    in_sem,
    packed_sem,
    sums_sem,
):
    regular, spare = shares_of(capacity)
    clusters = sums_ref.shape[0]
    block_count, rows = order_ref.shape
    tall = STEP_BLOCKS * rows

    def load(step):
        span = pl.ds(pl.multiple_of(step * tall, tall), tall)
        return pltpu.make_async_copy(x_ref.at[span], x_buf.at[span], in_sem.at[step])

    def store_packed(c):
        span = pl.ds(c * capacity, capacity)
        return pltpu.make_async_copy(packed_buf.at[span], packed_ref.at[span], packed_sem.at[c])

    def store_sums(c):
        return pltpu.make_async_copy(sums_buf.at[c], sums_ref.at[c], sums_sem.at[c])

    def clear(c):
        count_ref[c] = 0
        sums_buf[c] = jnp.zeros(sums_buf.shape[1:], jnp.float32)
        for j in range(capacity):
            packed_buf[c * capacity + j] = jnp.zeros(packed_buf.shape[1:], jnp.bfloat16)

    run(block_count // STEP_BLOCKS, lambda step: load(step).start())
    run(clusters, clear)
    extra_ref[...] = jnp.zeros(extra_ref.shape, jnp.bfloat16)
    table_row = lax.broadcasted_iota(jnp.int32, table_ref.shape, 0)
    table_col = lax.broadcasted_iota(jnp.int32, table_ref.shape, 1)
    table_ref[...] = jnp.where(table_row == 0, -1, 0)
    count_ref[clusters] = 0
    source = lax.broadcasted_iota(jnp.int32, (rows, rows), 0)

    def work(step):
        load(step).wait()
        x = x_buf[pl.ds(pl.multiple_of(step * tall, tall), tall), :]
        order = order_ref[pl.ds(pl.multiple_of(step * STEP_BLOCKS, STEP_BLOCKS), STEP_BLOCKS), :]
        sketched = jnp.dot(x, sketch_ref[...], preferred_element_type=jnp.float32).astype(
            jnp.bfloat16
        )
        for i in range(STEP_BLOCKS):
            cluster = map_ref[step * STEP_BLOCKS + i]
            rank = count_ref[cluster]
            count_ref[cluster] = rank + 1
            block = sketched[i * rows : (i + 1) * rows]
            taken = jnp.where(source == order[i : i + 1, :], 1.0, 0.0).astype(jnp.bfloat16)
            slot = cluster * capacity + rank
            moved = dot_first(taken, block).astype(jnp.bfloat16)
            packed_buf[slot] = moved
            if spare:
                over = rank >= regular
                seen = count_ref[clusters]
                place = jnp.where(over, jnp.minimum(seen, spare), spare)
                count_ref[clusters] = seen + jnp.where(over, 1, 0)
                extra_ref[place] = moved
                here = (table_row == 0) & (table_col == place) & (place < spare)
                table_ref[...] = jnp.where(here, slot, table_ref[...])
            wide = jnp.concatenate([block, x[i * rows : (i + 1) * rows, :]], axis=1)
            sums_buf[cluster] += dot_first(block, wide)

    run(block_count // STEP_BLOCKS, work)
    excess = jnp.where(count_ref[clusters] > spare, 1, 0)
    table_ref[...] = jnp.where(table_row == 1, excess, table_ref[...])
    run(clusters, lambda c: store_sums(c).start())
    run(clusters, lambda c: store_packed(c).start())
    run(clusters, lambda c: store_sums(c).wait())
    run(clusters, lambda c: store_packed(c).wait())


def flip(index, mask):
    return index + mask - 2 * mask * lax.rem(lax.div(index, mask), 2)


def exchange_kernel(
    capacity,
    row_norm,
    leaves,
    lines,
    packed_ref,
    sums_ref,
    level_ref,
    extra_ref,
    table_ref,
    received_ref,
    inverse_ref,
    transfers_ref,
    summary_ref,
    extras_ref,
    tables_ref,
    excess_ref,
    *scratch,
):
    rounds = lines.bit_length() - 1
    halves = scratch[:rounds]
    partial = scratch[rounds : 2 * rounds]
    (
        landed,
        whole,
        nodes,
        siblings,
        block_send,
        block_recv,
        half_send,
        half_recv,
        leaf_send,
        leaf_recv,
        line_send,
        line_recv,
        node_send,
        node_recv,
        own_sem,
        excesses,
        table_send,
        table_recv,
        excess_send,
        excess_recv,
        extra_send,
        extra_recv,
    ) = scratch[2 * rounds :]
    regular, spare = shares_of(capacity)
    me = lax.axis_index("leaf")
    line = lax.axis_index("rows")
    rank = inverse_ref.shape[0]
    sample_cols = level_ref.shape[1]

    barrier = pltpu.get_barrier_semaphore()
    for d in range(1, leaves):
        pl.semaphore_signal(
            barrier, inc=1, device_id=(lax.rem(me + d, leaves), line), device_id_type=MESH
        )
    for d in range(1, lines):
        pl.semaphore_signal(
            barrier, inc=1, device_id=(me, lax.rem(line + d, lines)), device_id_type=MESH
        )
    pl.semaphore_wait(barrier, leaves + lines - 2)

    def remote(src, dst, send, recv, target):
        copy = pltpu.make_async_remote_copy(
            src_ref=src,
            dst_ref=dst,
            send_sem=send,
            recv_sem=recv,
            device_id=target,
            device_id_type=MESH,
        )
        copy.start()
        return copy

    pieces = max(1, regular // 4)
    depth = regular // pieces
    chunks = (leaves - 1) * pieces
    per = max(1, chunks // 21)
    first = min(chunks, 4 * per)

    def chunk(i):
        d = 1 + lax.rem(i, leaves - 1)
        offset = lax.div(i, leaves - 1) * depth
        peer = lax.rem(me + d, leaves)
        return pltpu.make_async_remote_copy(
            src_ref=packed_ref.at[pl.ds(peer * capacity + offset, depth)],
            dst_ref=received_ref.at[pl.ds(me * capacity + offset, depth)],
            send_sem=block_send.at[i],
            recv_sem=block_recv.at[i],
            device_id=(peer, line),
            device_id_type=MESH,
        )

    def send_chunks(base, count):
        if count == 0:
            return
        run(count, lambda i: chunk(base + i).start())

    half = leaves // 2
    mirror = lax.rem(me + half, leaves)
    base_leaf = lax.div(me, half) * half
    others = [base_leaf + lax.rem(me - base_leaf + d, half) for d in range(1, half)]
    spares, tables = [], []
    if spare:
        stock = extra_ref.at[pl.ds(0, spare)]
        crossing = remote(
            stock, extras_ref.at[me], extra_send.at[0], extra_recv.at[0], (mirror, line)
        )
        for d, other in enumerate(others, 1):
            spares.append(
                remote(
                    stock, extras_ref.at[me], extra_send.at[d], extra_recv.at[d], (other, line)
                )
            )
        own_extra = pltpu.make_async_copy(stock, extras_ref.at[me], extra_send.at[2 * half])
        own_extra.start()
        tables_ref[me] = table_ref[...]
        for d in range(1, leaves):
            tables.append(
                remote(
                    table_ref,
                    tables_ref.at[me],
                    table_send.at[d],
                    table_recv.at[d],
                    (lax.rem(me + d, leaves), line),
                )
            )
    send_chunks(0, first)

    held, start, size = sums_ref, 0, rank
    for k in range(rounds):
        mask = 2**k
        size //= 2
        side = lax.rem(lax.div(line, mask), 2)
        copy = remote(
            held.at[:, pl.ds(pl.multiple_of((1 - side) * size, size), size), :],
            halves[k],
            half_send.at[k],
            half_recv.at[k],
            (me, flip(line, mask)),
        )
        if k == 0:
            own = pltpu.make_async_copy(
                packed_ref.at[pl.ds(me * capacity, regular)],
                received_ref.at[pl.ds(me * capacity, regular)],
                own_sem,
            )
            own.start()
        copy.wait()
        kept = pl.multiple_of(side * size, size)
        for c in range(leaves):
            partial[k][c] = held[c, pl.ds(kept, size), :] + halves[k][c]
        held, start = partial[k], start + side * size

    sums = []
    for d in range(1, leaves):
        peer = lax.rem(me + d, leaves)
        sums.append(
            remote(held.at[peer], landed.at[me], leaf_send.at[d], leaf_recv.at[d], (peer, line))
        )
    total = held[me]
    for d in range(1, leaves):
        sums[d - 1].wait()
        total = total + landed[lax.rem(me - d + leaves, leaves)]
    start = pl.multiple_of(start, size)
    whole[pl.ds(start, size), :] = total
    shares = [
        remote(
            whole.at[pl.ds(start, size), :],
            whole.at[pl.ds(start, size), :],
            line_send.at[d],
            line_recv.at[d],
            (me, lax.rem(line + d, lines)),
        )
        for d in range(1, lines)
    ]
    for copy in shares:
        copy.wait()
    if spare:
        crossing.wait()
        for d, other in enumerate(others, 1):
            spares.append(
                remote(
                    extras_ref.at[mirror],
                    extras_ref.at[mirror],
                    extra_send.at[half + d],
                    extra_recv.at[half + d],
                    (other, line),
                )
            )

    eye = identity(rank)
    base = first
    inverse = inverse_factor(
        whole[:, :rank] / row_norm + SHIFT * eye,
        lambda i, base=base: send_chunks(base + i * per, per if i < 3 else 0),
    )
    base += 3 * per
    inverse_ref[...] = inverse
    nodes[0] = jnp.dot(inverse, whole[:, rank:], precision=HIGHEST) * (
        math.sqrt(sample_cols) / row_norm
    )
    for t in range(LEVELS):
        copy = remote(
            nodes.at[t], siblings.at[t], node_send.at[t], node_recv.at[t], (flip(me, 2**t), line)
        )
        own_node = nodes[t]
        sketch = level_ref[t]
        projected = jnp.dot(own_node, sketch, precision=HIGHEST)
        wide = jnp.concatenate([projected, own_node], axis=1)
        own_product = dot_first(projected, wide, HIGHEST)
        copy.wait()
        if t == LEVELS - 1:
            send_chunks(base, chunks - base)
        parts = (3, 2, 0)[t]
        other_node = siblings[t]
        other = jnp.dot(other_node, sketch, precision=HIGHEST)
        other_wide = jnp.concatenate([other, other_node], axis=1)
        product = own_product + dot_first(other, other_wide, HIGHEST)
        inverse = inverse_factor(
            product[:, :rank] / (2 * rank) + SHIFT * eye,
            lambda i, base=base, parts=parts: send_chunks(base + i * per, per if i < parts else 0),
        )
        base += parts * per
        transfers_ref[t] = dot_last(projected, inverse, HIGHEST)
        parent = jnp.dot(inverse, product[:, rank:], precision=HIGHEST) * (
            math.sqrt(sample_cols) / (2 * rank)
        )
        if t == LEVELS - 1:
            summary_ref[...] = parent
        else:
            nodes[t + 1] = parent

    if spare:
        for copy in tables:
            copy.wait()
        excess = tables_ref[0]
        for c in range(1, leaves):
            excess = jnp.maximum(excess, tables_ref[c])
        excesses[line] = excess
        flags = [
            remote(
                excesses.at[line],
                excesses.at[line],
                excess_send.at[d],
                excess_recv.at[d],
                (me, lax.rem(line + d, lines)),
            )
            for d in range(1, lines)
        ]
        for copy in flags:
            copy.wait()
        excess = excesses[0]
        for r in range(1, lines):
            excess = jnp.maximum(excess, excesses[r])
        excess_ref[...] = excess
        own_extra.wait()
        for copy in spares:
            copy.wait()
    else:
        tables_ref[...] = jnp.zeros(tables_ref.shape, jnp.int32)
        excess_ref[...] = jnp.zeros(excess_ref.shape, jnp.int32)
    own.wait()
    run(chunks, lambda i: chunk(i).wait())


def basis_kernel(rows_ref, inverse_ref, basis_ref, in_buf, out_buf, in_sem, out_sem):
    tall = rows_ref.shape[0] // BASIS_PARTS

    def span(i):
        return pl.ds(pl.multiple_of(i * tall, tall), tall)

    def load(i):
        return pltpu.make_async_copy(rows_ref.at[span(i)], in_buf.at[span(i)], in_sem.at[i])

    def store(i):
        return pltpu.make_async_copy(out_buf.at[span(i)], basis_ref.at[span(i)], out_sem.at[i])

    run(BASIS_PARTS, lambda i: load(i).start())
    inverse = inverse_ref[...]
    upper = inverse.astype(jnp.bfloat16)
    lower = (inverse - upper.astype(jnp.float32)).astype(jnp.bfloat16)
    both = jnp.concatenate([upper.T, lower.T], axis=0)

    def work(i):
        load(i).wait()
        rows = in_buf[span(i), :]
        twice = jnp.concatenate([rows, rows], axis=1)
        out_buf[span(i), :] = jnp.dot(twice, both, preferred_element_type=jnp.float32).astype(
            jnp.bfloat16
        )
        store(i).start()

    run(BASIS_PARTS, work)
    run(BASIS_PARTS, lambda i: store(i).wait())


def spread_kernel(
    capacity, tables_ref, rows_ref, extras_ref, inverse_ref, basis_ref, in_buf, out_buf,
    in_sem, extra_sem, out_sem,
):
    regular, spare = shares_of(capacity)
    me = lax.axis_index("leaf")
    leaves = rows_ref.shape[0] // capacity
    rows, rank = rows_ref.shape[1:]

    def load(c):
        span = pl.ds(c * capacity, regular)
        return pltpu.make_async_copy(rows_ref.at[span], in_buf.at[span], in_sem.at[c])

    def store(c):
        span = pl.ds(c * capacity, capacity)
        return pltpu.make_async_copy(out_buf.at[span], basis_ref.at[span], out_sem.at[c])

    def patch(c, e, act):
        slot = tables_ref[c, 0, e]

        @pl.when((slot >= me * capacity) & (slot < (me + 1) * capacity))
        def _():
            act(
                pltpu.make_async_copy(
                    extras_ref.at[c, e],
                    in_buf.at[c * capacity + slot - me * capacity],
                    extra_sem.at[c, e],
                )
            )

    run(leaves, lambda c: load(c).start())
    inverse = inverse_ref[...]
    upper = inverse.astype(jnp.bfloat16)
    lower = (inverse - upper.astype(jnp.float32)).astype(jnp.bfloat16)
    both = jnp.concatenate([upper.T, lower.T], axis=0)

    def begin(c):
        span = pl.ds(c * capacity + regular, capacity - regular)
        in_buf[span] = jnp.zeros((capacity - regular, rows, rank), jnp.bfloat16)
        for e in range(spare):
            patch(c, e, lambda copy: copy.start())

    run(leaves, begin)

    def work(c):
        load(c).wait()
        for e in range(spare):
            patch(c, e, lambda copy: copy.wait())
        blocks = in_buf[pl.ds(c * capacity, capacity)].reshape(capacity * rows, rank)
        twice = jnp.concatenate([blocks, blocks], axis=1)
        bases = jnp.dot(twice, both, preferred_element_type=jnp.float32).astype(jnp.bfloat16)
        out_buf[pl.ds(c * capacity, capacity)] = bases.reshape(capacity, rows, rank)
        store(c).start()

    run(leaves, work)
    run(leaves, lambda c: store(c).wait())


def body(samples, row_order, cluster_map, leaf_sketch, level_sketch):
    block_count = cluster_map.shape[0]
    block_rows = row_order.shape[1]
    sample_cols = samples.shape[1]
    rank = leaf_sketch.shape[1]
    leaves = lax.axis_size("leaf")
    lines = lax.axis_size("rows")
    capacity = 2 * block_count // leaves
    slots = leaves * capacity
    width = rank + sample_cols
    row_norm = float(lines * block_count * block_rows)
    vmem = pl.BlockSpec(memory_space=pltpu.VMEM)
    anywhere = pl.BlockSpec(memory_space=pl.ANY)
    dma = pltpu.SemaphoreType.DMA

    regular, spare = shares_of(capacity)
    table = jax.ShapeDtypeStruct((8, 128), jnp.int32)
    packed, sums, extra, own_table = pl.pallas_call(
        functools.partial(local_kernel, capacity),
        in_specs=[pl.BlockSpec(memory_space=pltpu.SMEM), vmem, anywhere, vmem],
        out_specs=[anywhere, anywhere, vmem, vmem],
        out_shape=[
            jax.ShapeDtypeStruct((slots, block_rows, rank), jnp.bfloat16),
            jax.ShapeDtypeStruct((leaves, rank, width), jnp.float32),
            jax.ShapeDtypeStruct((spare + 1, block_rows, rank), jnp.bfloat16),
            table,
        ],
        scratch_shapes=[
            pltpu.VMEM((block_count * block_rows, sample_cols), jnp.bfloat16),
            pltpu.VMEM((slots, block_rows, rank), jnp.bfloat16),
            pltpu.VMEM((leaves, rank, width), jnp.float32),
            pltpu.SMEM((leaves + 1,), jnp.int32),
            dma((block_count // STEP_BLOCKS,)),
            dma((leaves,)),
            dma((leaves,)),
        ],
        compiler_params=pltpu.CompilerParams(vmem_limit_bytes=VMEM_BYTES),
        name="sketch_blocks",
    )(cluster_map, row_order, samples, leaf_sketch)

    rounds = lines.bit_length() - 1
    shares = [
        pltpu.VMEM((leaves, rank >> (k + 1), width), jnp.float32) for k in range(rounds)
    ]
    chunks = (leaves - 1) * max(1, regular // 4)
    received, inverse, transfers, summary, extras, tables, excess = pl.pallas_call(
        functools.partial(exchange_kernel, capacity, row_norm, leaves, lines),
        in_specs=[anywhere, vmem, vmem, anywhere, vmem],
        out_specs=[anywhere, vmem, vmem, vmem, anywhere, vmem, vmem],
        out_shape=[
            jax.ShapeDtypeStruct((slots, block_rows, rank), jnp.bfloat16),
            jax.ShapeDtypeStruct((rank, rank), jnp.float32),
            jax.ShapeDtypeStruct((LEVELS, rank, rank), jnp.float32),
            jax.ShapeDtypeStruct((rank, sample_cols), jnp.float32),
            jax.ShapeDtypeStruct((leaves, max(spare, 1), block_rows, rank), jnp.bfloat16),
            jax.ShapeDtypeStruct((leaves, 8, 128), jnp.int32),
            table,
        ],
        scratch_shapes=[
            *shares,
            *shares,
            pltpu.VMEM((leaves, rank // lines, width), jnp.float32),
            pltpu.VMEM((rank, width), jnp.float32),
            pltpu.VMEM((LEVELS, rank, sample_cols), jnp.float32),
            pltpu.VMEM((LEVELS, rank, sample_cols), jnp.float32),
            dma((chunks,)),
            dma((chunks,)),
            dma((rounds,)),
            dma((rounds,)),
            dma((leaves,)),
            dma((leaves,)),
            dma((lines,)),
            dma((lines,)),
            dma((LEVELS,)),
            dma((LEVELS,)),
            dma,
            pltpu.VMEM((lines, 8, 128), jnp.int32),
            dma((leaves,)),
            dma((leaves,)),
            dma((lines,)),
            dma((lines,)),
            dma((leaves + 1,)),
            dma((leaves + 1,)),
        ],
        compiler_params=pltpu.CompilerParams(
            collective_id=0, has_side_effects=True, vmem_limit_bytes=VMEM_BYTES
        ),
        name="exchange_and_merge",
    )(packed, sums, level_sketch, extra, own_table)

    total_rows = slots * block_rows

    def all_slots(full):
        return pl.pallas_call(
            basis_kernel,
            in_specs=[anywhere, vmem],
            out_specs=anywhere,
            out_shape=jax.ShapeDtypeStruct((total_rows, rank), jnp.bfloat16),
            scratch_shapes=[
                pltpu.VMEM((total_rows, rank), jnp.bfloat16),
                pltpu.VMEM((total_rows, rank), jnp.bfloat16),
                dma((BASIS_PARTS,)),
                dma((BASIS_PARTS,)),
            ],
            compiler_params=pltpu.CompilerParams(vmem_limit_bytes=VMEM_BYTES),
            name="leaf_bases",
        )(full.reshape(total_rows, rank), inverse)

    def send_again():
        return all_slots(lax.all_to_all(packed, "leaf", split_axis=0, concat_axis=0, tiled=True))

    def spread():
        return pl.pallas_call(
            functools.partial(spread_kernel, capacity),
            in_specs=[pl.BlockSpec(memory_space=pltpu.SMEM), anywhere, anywhere, vmem],
            out_specs=anywhere,
            out_shape=jax.ShapeDtypeStruct((slots, block_rows, rank), jnp.bfloat16),
            scratch_shapes=[
                pltpu.VMEM((slots, block_rows, rank), jnp.bfloat16),
                pltpu.VMEM((slots, block_rows, rank), jnp.bfloat16),
                dma((leaves,)),
                dma((leaves, spare)),
                dma((leaves,)),
            ],
            compiler_params=pltpu.CompilerParams(vmem_limit_bytes=VMEM_BYTES),
            name="spread_bases",
        )(tables, received, extras, inverse).reshape(total_rows, rank)

    if spare:
        basis = lax.cond(excess[1, 0] > 0, send_again, spread)
    else:
        basis = all_slots(received)
    return basis, transfers[None], summary[None]


def solution(mesh):
    in_specs = (P(("leaf", "rows"), None), P(("leaf", "rows"), None), P(("leaf", "rows")), P(), P())
    out_specs = (P(("leaf", "rows"), None), P("leaf", None, None, None), P("leaf", None, None))
    return jax.shard_map(body, mesh=mesh, in_specs=in_specs, out_specs=out_specs, check_vma=False)
```
